256 devices in a mesh: grp: 8 (over x, y_hi), row: 4 (over y_lo, core), col: 8 (over z).
Axes of the slice: x: 4, y: 4 (y_hi: 2, y_lo: 2; y = y_hi * 2 + y_lo), z: 8, core: 2. Of those that a mesh axis runs over, the one named last changes fastest.
Arguments:
- phase: bfloat16 [64, 8, 128, 4096], P('grp', None, 'row', 'col'), may hold values from -6 to 6
- pseudo_inverse: bfloat16 [48, 64], replicated, may hold values from -0.75 to 0.75
- rotation: float32 [4, 3], replicated, may hold values from -4 to 4
- plate_id: int32 [1024, 4096], P(('grp', 'row'), 'col'), may hold values from 0 to 3
- coherent: int32 [1024, 4096], P(('grp', 'row'), 'col'), may hold values 0 or 1
Outputs:
- displacement: bfloat16 [48, 1024, 4096], P(None, ('grp', 'row'), 'col')
- grad_rows: float32 [1024, 4096], P(('grp', 'row'), 'col')
- grad_cols: float32 [1024, 4096], P(('grp', 'row'), 'col')
The draws below stay inside these ranges and needn't reach their ends.
All inputs are finite; a program needn't handle non-finite values. No bound on the sum of `coherent` on one device may be relied on, other than what follows from the above.
Results may differ from the reference program's by a relative error of at most 0.001.
Values may be sent and summed in bfloat16 or wider, within the bound.
No kernel may reach another device: no remote copies, remote signals or barrier semaphores. Data moves between devices by JAX's collectives and lax.ppermute only.
A program may use at most 128 MiB of HBM per device.

```python
import jax
import jax.numpy as jnp
from jax import lax

IFG = 64
EPOCHS = 48
PLATES = 4
HALF = 16
CY = 32
NY = 1024
NX = 4096
BAND = 128
N_GRP = 8
N_ROW = 4


def with_ends(entries, own_key, least, top_value):
    dims = entries.shape
    spot = [jax.random.randint(jax.random.fold_in(own_key, axis), (), 0, dims[axis]) for axis in range(len(dims))]
    entries = entries.at[tuple(spot)].set(least)
    longest = dims.index(max(dims))
    spot[longest] = (spot[longest] + 1) % dims[longest]
    return entries.at[tuple(spot)].set(top_value)


def steps_of(rng, dims, pieces, least, high):
    def one(position, parts):
        heights = jax.random.uniform(jax.random.fold_in(jax.random.fold_in(rng, 6), position), (parts,), jnp.float32, least / len(pieces), high / len(pieces))
        return jnp.repeat(jnp.exp(heights), dims[position] // parts).reshape((-1,) + (1,) * (len(dims) - position - 1))

    factor_of = one(*pieces[0])
    for cut in pieces[1:]:
        factor_of = factor_of * one(*cut)
    return factor_of


def noise(key, dims, deviation, reach, cuts=(), held_as=jnp.bfloat16):
    entries = deviation * jax.random.normal(key, dims, jnp.float32)
    if cuts:
        entries = entries * steps_of(key, dims, cuts, -0.22, 0.18)
    return jnp.clip(entries, -reach, reach).astype(held_as)


def setup_inputs(seed: int = 0) -> dict:
    splits = jax.random.split(jax.random.key(seed), 6)
    phase = noise(splits[0], (IFG, N_GRP, BAND, NX), 1.0, 6.0, ((0, 8), (2, 4), (3, 8)))
    pseudo_inverse = noise(splits[1], (EPOCHS, IFG), IFG ** -0.5, 0.75)
    rotation = noise(splits[2], (PLATES, 3), 1.0, 4.0, (), jnp.float32)
    plate_id = with_ends(jax.random.randint(splits[3], (NY, NX), 0, PLATES), jax.random.fold_in(splits[3], 1), 0, PLATES - 1).astype(jnp.int32)
    coherent = with_ends((jax.random.randint(splits[4], (NY, NX), 0, 4) < 3).astype(jnp.int32), jax.random.fold_in(splits[4], 1), 0, 1)
    return {"phase": phase, "pseudo_inverse": pseudo_inverse, "rotation": rotation, "plate_id": plate_id, "coherent": coherent}


def lever_field(rows, cols):
    lat = jnp.deg2rad(36.0 + 6.0 * (rows + 0.5) / NY)
    lon = jnp.deg2rad(26.0 + 19.0 * (cols + 0.5) / NX)
    px = jnp.cos(lat) * jnp.cos(lon)
    py = jnp.cos(lat) * jnp.sin(lon)
    pz = jnp.sin(lat) + 0.0 * lon
    sx, sy, sz = (0.38, -0.08, 0.92)
    return jnp.stack([py * sz - pz * sy, pz * sx - px * sz, px * sy - py * sx])

def slope_weights():
    steps = jnp.arange(EPOCHS, dtype=jnp.float32) - (EPOCHS - 1) / 2.0
    return steps / jnp.sqrt(jnp.sum(steps * steps))

def reference(phase, pseudo_inverse, rotation, plate_id, coherent):
    bands = N_GRP * N_ROW
    stack = phase.reshape(IFG, bands, CY, NX)
    slope = slope_weights()
    inverse = pseudo_inverse.astype(jnp.float32)

    def one_band(index):
        piece = lax.dynamic_index_in_dim(stack, index, 1, keepdims=False).astype(jnp.float32)
        series = jnp.einsum('ei,iyx->eyx', inverse, piece)
        rate = jnp.einsum('e,eyx->yx', slope, series, precision=lax.Precision.HIGHEST)
        return (series.astype(jnp.bfloat16), rate)
    series_all, rate_all = lax.map(one_band, jnp.arange(bands, dtype=jnp.int32))
    displacement = jnp.transpose(series_all, (1, 0, 2, 3)).reshape(EPOCHS, NY, NX)
    rate = rate_all.reshape(NY, NX)
    rows = jnp.arange(NY, dtype=jnp.float32)[:, None]
    cols = jnp.arange(NX, dtype=jnp.float32)[None, :]
    lever = lever_field(rows, cols)
    plate_rate = jnp.zeros((NY, NX), jnp.float32)
    for plate in range(PLATES):
        along = rotation[plate, 0] * lever[0] + rotation[plate, 1] * lever[1] + rotation[plate, 2] * lever[2]
        plate_rate = plate_rate + jnp.where(plate_id == plate, along, 0.0)
    velocity = coherent.astype(jnp.float32) * rate - plate_rate
    norm = jnp.sqrt(jnp.float32(HALF * (HALF + 1) * (2 * HALF + 1) // 3))
    padded = jnp.pad(velocity, HALF)
    grad_rows = jnp.zeros((NY, NX), jnp.float32)
    grad_cols = jnp.zeros((NY, NX), jnp.float32)
    for k in range(-HALF, HALF + 1):
        tap = k / norm
        grad_rows = grad_rows + tap * padded[HALF + k:HALF + k + NY, HALF:HALF + NX]
        grad_cols = grad_cols + tap * padded[HALF:HALF + NY, HALF + k:HALF + k + NX]
    return (displacement, grad_rows, grad_cols)
```

```python
import jax
import jax.numpy as jnp
from jax import lax
from jax.experimental import pallas as pl
from jax.experimental.pallas import tpu as pltpu
from jax.sharding import PartitionSpec as P

REACH = 16
SUB = 16
LANES = 128
F32 = jnp.float32
BF16 = jnp.bfloat16
VMEM_BYTES = 48 << 20

FLOWS = {
    "own": (0, 0),
    "D2": (2, 1),
    "Da": ("a", 1),
    "Db": ("b", 1),
    "X2": (2, 0),
    "Y2": (0, 1),
    "Xa": ("a", 0),
    "Xb": ("b", 0),
}
EMIT = ("Xa", "Da", "Y2", "X2", "Db", "Xb", "D2")


def along_x(step, x, core, pick):
    if step == "a":
        return pick(((x + core) & 1) == 0, 1, 3)
    if step == "b":
        return pick(((x + core) & 1) == 0, 3, 1)
    return step


def partner(flow, x, y, core, pick):
    step, turn = FLOWS[flow]
    return (((x + along_x(step, x, core, pick)) & 3) << 1) + ((y + turn) & 1)


def swap_pairs(flow):
    def choose(test, first, second):
        return first if test else second

    pairs = []
    for grp in range(8):
        for row in range(4):
            other = partner(flow, grp // 2, grp % 2, row % 2, choose)
            pairs.append((grp * 4 + row, other * 4 + row))
    return pairs


def row_pairs(tiles, first):
    pairs = []
    for low in range(first, tiles - 1, 2):
        pairs += [(low, low + 1), (low + 1, low)]
    return pairs


def prep_kernel(src_ref, rot_ref, pinv_ref, lat_ref, lon_ref, plate_ref, w_ref, rate_ref):
    epochs, ifg = pinv_ref.shape
    tall = epochs * SUB
    grow = lax.broadcasted_iota(jnp.int32, (tall, epochs), 0) // SUB
    pick = (grow == lax.broadcasted_iota(jnp.int32, (tall, epochs), 1)).astype(BF16)
    tall_inverse = jnp.dot(pick, pinv_ref[...], preferred_element_type=F32).astype(BF16)
    share = ifg // 8
    wide = share * SUB
    here = lax.broadcasted_iota(jnp.int32, (ifg, wide), 0)
    there = lax.broadcasted_iota(jnp.int32, (ifg, wide), 1) // SUB
    diagonal = (lax.broadcasted_iota(jnp.int32, (tall, wide), 0) % SUB) == (
        lax.broadcasted_iota(jnp.int32, (tall, wide), 1) % SUB
    )
    for k in range(8):
        spread = (here == there + src_ref[k] * share).astype(BF16)
        block = jnp.dot(tall_inverse, spread, preferred_element_type=F32)
        w_ref[:, k * wide : (k + 1) * wide] = jnp.where(diagonal, block, 0.0).astype(BF16)
    sx, sy, sz = (0.38, -0.08, 0.92)
    cos_lat, sin_lat = lat_ref[:, 0:1], lat_ref[:, 1:2]
    cos_lon, sin_lon = lon_ref[0:1, :], lon_ref[1:2, :]
    px = cos_lat * cos_lon
    py = cos_lat * sin_lon
    pz = sin_lat + 0.0 * sin_lon
    lever = (py * sz - pz * sy, pz * sx - px * sz, px * sy - py * sx)
    plate = plate_ref[...]
    total = jnp.zeros(plate.shape, F32)
    for p in range(rot_ref.shape[0]):
        along = rot_ref[p, 0] * lever[0] + rot_ref[p, 1] * lever[1] + rot_ref[p, 2] * lever[2]
        total = total + jnp.where(plate == p, along, 0.0)
    rate_ref[...] = total


def rate_kernel(src_ref, weight_ref, place_ref, *refs):
    blocks, (coherent_ref, plate_rate_ref), outs = refs[:8], refs[8:10], refs[10:]
    v_ref, one_ref, two_ref, left_ref, right_ref = outs
    share, rows, cols = blocks[0].shape
    rate = jnp.zeros((rows, cols), F32)
    for k, block in enumerate(blocks):
        for i in range(share):
            rate = rate + weight_ref[src_ref[k] * share + i] * block[i].astype(F32)
    v_ref[...] = coherent_ref[...].astype(F32) * rate - plate_rate_ref[...]
    core, column = place_ref[0], place_ref[1]
    top, low = v_ref[:REACH, :], v_ref[rows - REACH :, :]
    first, last = v_ref[:, :LANES], v_ref[:, cols - LANES :]
    one_ref[...] = jnp.where(core == 0, low, top)
    two_ref[...] = jnp.where(core == 0, top, low)
    left_ref[...] = jnp.where(column == 0, last, first)
    right_ref[...] = jnp.where(column == 0, first, last)


def product_kernel(w_ref, *refs):
    blocks, out_ref = refs[:-1], refs[-1]
    share, rows, cols = blocks[0].shape
    epochs = out_ref.shape[0]
    for t in range(rows // SUB):
        part = slice(t * SUB, (t + 1) * SUB)
        stack = jnp.concatenate([b[:, part, :].reshape(share * SUB, cols) for b in blocks], axis=0)
        series = jnp.dot(w_ref[...], stack, preferred_element_type=F32)
        out_ref[:, part, :] = series.astype(BF16).reshape(epochs, SUB, cols)


def three_parts(value):
    high = value.astype(BF16)
    rest = value - high.astype(F32)
    mid = rest.astype(BF16)
    low = (rest - mid.astype(F32)).astype(BF16)
    return high, mid, low


def banded(shape, axis, start):
    step = lax.broadcasted_iota(jnp.int32, shape, axis) - start
    step = step - lax.broadcasted_iota(jnp.int32, shape, 1 - axis)
    return jnp.where(jnp.abs(step) <= REACH, step, 0).astype(F32).astype(BF16)


def gradient_kernel(place_ref, v_ref, one_ref, two_ref, left_ref, right_ref, rows_ref, cols_ref):
    rows, cols = v_ref.shape
    scale = (REACH * (REACH + 1) * (2 * REACH + 1) // 3) ** -0.5
    core, column = place_ref[0], place_ref[1]
    v = v_ref[...]
    one, two = one_ref[...], two_ref[...]
    above = jnp.where(core == 0, two, one)
    below = jnp.where(core == 0, one, two)
    upright = jnp.concatenate([above, v, below], axis=0)
    taps = banded((rows, rows + 2 * REACH), 1, REACH)
    total = jnp.zeros((rows, cols), F32)
    for part in three_parts(upright):
        total = total + jnp.dot(taps, part, preferred_element_type=F32)
    rows_ref[...] = total * scale
    first, second = left_ref[...], right_ref[...]
    before = jnp.where(column == 0, second, first)
    after = jnp.where(column == 0, first, second)
    sideways = jnp.concatenate([before, v, after], axis=1)
    parts = jnp.concatenate(three_parts(sideways), axis=0)
    taps = banded((3 * LANES, LANES), 0, LANES)
    for c in range(0, cols, LANES):
        found = jnp.dot(parts[:, c : c + 3 * LANES], taps, preferred_element_type=F32)
        found = found[:rows] + found[rows : 2 * rows] + found[2 * rows :]
        cols_ref[:, c : c + LANES] = found * scale


SMEM = pl.BlockSpec(memory_space=pltpu.SMEM)
VMEM = pl.BlockSpec(memory_space=pltpu.VMEM)


def call(kernel, inputs, outputs, flops, moved, **more):
    return pl.pallas_call(
        kernel,
        in_specs=inputs,
        out_shape=outputs,
        cost_estimate=pl.CostEstimate(flops=flops, bytes_accessed=moved, transcendentals=0),
        compiler_params=pltpu.CompilerParams(vmem_limit_bytes=VMEM_BYTES),
        **more,
    )


def shape(*dims, dtype=F32):
    return jax.ShapeDtypeStruct(dims, dtype)


def on_device(phase, pseudo_inverse, rotation, plate_id, coherent):
    share, groups, rows, cols = phase.shape
    epochs, ifg = pseudo_inverse.shape
    grp, row, col = lax.axis_index("grp"), lax.axis_index("row"), lax.axis_index("col")
    x, y, core = grp >> 1, grp & 1, row & 1
    tiles = groups * lax.axis_size("row")
    total_rows, total_cols = tiles * rows, lax.axis_size("col") * cols

    names = ("own",) + EMIT
    sources = {name: partner(name, x, y, core, jnp.where) for name in names}
    blocks = {}
    for name in names:
        block = lax.dynamic_index_in_dim(phase, sources[name], 1, keepdims=False)
        if name != "own":
            block = lax.ppermute(block, ("grp", "row"), swap_pairs(name))
        blocks[name] = block
    src = jnp.stack([sources[name] for name in names]).astype(jnp.int32)
    held = [blocks[name] for name in names]

    steps = jnp.arange(epochs, dtype=F32) - (epochs - 1) / 2.0
    slope = steps / jnp.sqrt(jnp.sum(steps * steps))
    weight = jnp.sum(slope[:, None] * pseudo_inverse.astype(F32), axis=0)
    tile = (grp * lax.axis_size("row") + row) * rows
    lat = jnp.deg2rad(36.0 + 6.0 * (tile.astype(F32) + jnp.arange(rows, dtype=F32) + 0.5) / total_rows)
    lon = jnp.deg2rad(26.0 + 19.0 * ((col * cols).astype(F32) + jnp.arange(cols, dtype=F32) + 0.5) / total_cols)
    lat = jnp.stack([jnp.cos(lat), jnp.sin(lat)], axis=1)
    lon = jnp.stack([jnp.cos(lon), jnp.sin(lon)], axis=0)
    place = jnp.stack([core, col & 1]).astype(jnp.int32)

    tall, deep = epochs * SUB, ifg * SUB
    w, plate_rate = call(
        prep_kernel,
        [SMEM, SMEM, VMEM, VMEM, VMEM, VMEM],
        (shape(tall, deep, dtype=BF16), shape(rows, cols)),
        2 * tall * deep * ifg,
        2 * tall * deep,
    )(src, rotation, pseudo_inverse, lat, lon, plate_id)

    velocity, one, two, left, right = call(
        rate_kernel,
        [SMEM, SMEM, SMEM] + [VMEM] * 10,
        (shape(rows, cols), shape(REACH, cols), shape(REACH, cols), shape(rows, LANES), shape(rows, LANES)),
        2 * ifg * rows * cols,
        2 * ifg * rows * cols,
    )(src, weight, place, *held, coherent, plate_rate)

    one = lax.ppermute(one, ("grp", "row"), row_pairs(tiles, 0))
    two = lax.ppermute(two, ("grp", "row"), row_pairs(tiles, 1))
    left = lax.ppermute(left, "col", row_pairs(lax.axis_size("col"), 0))
    right = lax.ppermute(right, "col", row_pairs(lax.axis_size("col"), 1))

    cut = 3
    displacement = call(
        product_kernel,
        [pl.BlockSpec((tall // cut, deep), lambda e: (e, 0))]
        + [pl.BlockSpec((share, rows, cols), lambda e: (0, 0, 0))] * 8,
        shape(epochs, rows, cols, dtype=BF16),
        2 * epochs * ifg * rows * cols * SUB,
        2 * (ifg + epochs) * rows * cols,
        grid=(cut,),
        out_specs=pl.BlockSpec((epochs // cut, rows, cols), lambda e: (e, 0, 0)),
    )(w, *held)

    grad_rows, grad_cols = call(
        gradient_kernel,
        [SMEM] + [VMEM] * 5,
        (shape(rows, cols), shape(rows, cols)),
        2 * 200 * rows * cols,
        16 * rows * cols,
    )(place, velocity, one, two, left, right)
    return (displacement, grad_rows, grad_cols)


def solution(mesh):
    return jax.shard_map(
        on_device,
        mesh=mesh,
        in_specs=(
            P("grp", None, "row", "col"),
            P(),
            P(),
            P(("grp", "row"), "col"),
            P(("grp", "row"), "col"),
        ),
        out_specs=(
            P(None, ("grp", "row"), "col"),
            P(("grp", "row"), "col"),
            P(("grp", "row"), "col"),
        ),
        check_vma=False,
    )
```

```python
import math

import jax
import jax.numpy as jnp
from jax import lax
from jax.experimental import pallas as pl
from jax.experimental.pallas import tpu as pltpu
from jax.sharding import PartitionSpec as P

REACH = 16
SUB = 16
LANES = 128
F32 = jnp.float32
BF16 = jnp.bfloat16
VMEM_BYTES = 40 << 20
CUT = 16

FLOWS = {
    "own": (0, 0),
    "D2": (2, 1),
    "Da": ("a", 1),
    "Db": ("b", 1),
    "X2": (2, 0),
    "Y2": (0, 1),
    "Xa": ("a", 0),
    "Xb": ("b", 0),
}
EARLY = ("D2", "Db")
LATE = ("X2", "Y2", "Da", "Xa", "Xb")
ORDER = ("own",) + EARLY + LATE
STARTS = EARLY + LATE


def along_x(step, x, core, pick):
    if step == "a":
        return pick(((x + core) & 1) == 0, 1, 3)
    if step == "b":
        return pick(((x + core) & 1) == 0, 3, 1)
    return step


def partner(flow, x, y, core, pick):
    step, turn = FLOWS[flow]
    return (((x + along_x(step, x, core, pick)) & 3) << 1) + ((y + turn) & 1)


def swap_pairs(flow):
    def choose(test, first, second):
        return first if test else second

    pairs = []
    for grp in range(8):
        for row in range(4):
            other = partner(flow, grp // 2, grp % 2, row % 2, choose)
            pairs.append((grp * 4 + row, other * 4 + row))
    return pairs


def ring_pairs(count, first):
    pairs = []
    for low in range(first, count, 2):
        high = (low + 1) % count
        pairs += [(low, high), (high, low)]
    return pairs


def three_parts(value):
    high = value.astype(BF16)
    rest = value - high.astype(F32)
    mid = rest.astype(BF16)
    low = (rest - mid.astype(F32)).astype(BF16)
    return high, mid, low


def rate_weights(pinv_ref, weight_ref):
    epochs, ifg = pinv_ref.shape
    steps = lax.broadcasted_iota(jnp.int32, (epochs, LANES), 0).astype(F32) - (epochs - 1) / 2.0
    slope = steps * (epochs * (epochs * epochs - 1) / 12.0) ** -0.5
    total = jnp.zeros((ifg, LANES), F32)
    for part in three_parts(slope):
        total = total + lax.dot_general(
            pinv_ref[...], part, (((0,), (0,)), ((), ())), preferred_element_type=F32
        )
    weight_ref[...] = total


def prep_kernel(rot_ref, pinv_ref, plate_ref, w_ref, rate_ref, weight_ref):
    rate_weights(pinv_ref, weight_ref)
    epochs, ifg = pinv_ref.shape
    rows, cols = plate_ref.shape
    x, y, core = place_here()
    tall = epochs * SUB
    grow = lax.broadcasted_iota(jnp.int32, (tall, epochs), 0) // SUB
    pick = (grow == lax.broadcasted_iota(jnp.int32, (tall, epochs), 1)).astype(BF16)
    tall_inverse = jnp.dot(pick, pinv_ref[...], preferred_element_type=F32).astype(BF16)
    share = ifg // 8
    wide = share * SUB
    here = lax.broadcasted_iota(jnp.int32, (ifg, wide), 0)
    there = lax.broadcasted_iota(jnp.int32, (ifg, wide), 1) // SUB
    diagonal = (lax.broadcasted_iota(jnp.int32, (tall, wide), 0) % SUB) == (
        lax.broadcasted_iota(jnp.int32, (tall, wide), 1) % SUB
    )
    for k, name in enumerate(ORDER):
        source = partner(name, x, y, core, jnp.where)
        spread = (here == there + source * share).astype(BF16)
        block = jnp.dot(tall_inverse, spread, preferred_element_type=F32)
        w_ref[:, k * wide : (k + 1) * wide] = jnp.where(diagonal, block, 0.0).astype(BF16)
    tile = lax.axis_index("grp") * lax.axis_size("row") + lax.axis_index("row")
    total_rows = rows * lax.axis_size("grp") * lax.axis_size("row")
    total_cols = cols * lax.axis_size("col")
    down = lax.broadcasted_iota(jnp.int32, (rows, LANES), 0) + tile * rows
    over = lax.broadcasted_iota(jnp.int32, (8, cols), 1) + lax.axis_index("col") * cols
    lat = (36.0 + 6.0 * (down.astype(F32) + 0.5) / total_rows) * (math.pi / 180.0)
    lon = (26.0 + 19.0 * (over.astype(F32) + 0.5) / total_cols) * (math.pi / 180.0)
    cos_lat, sin_lat = jnp.cos(lat)[:, 0:1], jnp.sin(lat)[:, 0:1]
    cos_lon, sin_lon = jnp.cos(lon)[0:1, :], jnp.sin(lon)[0:1, :]
    sx, sy, sz = (0.38, -0.08, 0.92)
    px = cos_lat * cos_lon
    py = cos_lat * sin_lon
    pz = sin_lat + 0.0 * sin_lon
    lever = (py * sz - pz * sy, pz * sx - px * sz, px * sy - py * sx)
    plate = plate_ref[...]
    total = jnp.zeros(plate.shape, F32)
    for p in range(rot_ref.shape[0]):
        along = jnp.zeros(plate.shape, F32)
        for k in range(3):
            along = along + rot_ref[p : p + 1, k : k + 1] * lever[k]
        total = total + jnp.where(plate == p, along, 0.0)
    rate_ref[...] = total


def weighted(total, block, weight_ref, source):
    share, _, cols = block.shape
    for i in range(share):
        row = weight_ref[pl.ds(source * share + i, 1), :]
        total = total + jnp.concatenate([row] * (cols // LANES), axis=1) * block[i].astype(F32)
    return total


def place_here():
    grp, row = lax.axis_index("grp"), lax.axis_index("row")
    return grp >> 1, grp & 1, row & 1


def rate_kernel(weight_ref, *refs):
    outs = refs[-5:]
    v_ref, one_ref, two_ref, left_ref, right_ref = outs
    coherent_ref, plate_rate_ref = refs[-7:-5]
    blocks = refs[:-7]
    rows, cols = v_ref.shape
    rate = jnp.zeros((rows, cols), F32)
    x, y, core = place_here()
    for name, block in zip(ORDER, blocks):
        rate = weighted(rate, block, weight_ref, partner(name, x, y, core, jnp.where))
    v_ref[...] = coherent_ref[...].astype(F32) * rate - plate_rate_ref[...]
    column = lax.axis_index("col") & 1
    top, low = v_ref[:REACH, :], v_ref[rows - REACH :, :]
    first, last = v_ref[:, :LANES], v_ref[:, cols - LANES :]
    one_ref[...] = jnp.where(core == 0, low, top)
    two_ref[...] = jnp.where(core == 0, top, low)
    left_ref[...] = jnp.where(column == 0, last, first)
    right_ref[...] = jnp.where(column == 0, first, last)


def stacked(blocks, part):
    share, _, cols = blocks[0].shape
    return jnp.concatenate([b[:, part, :].reshape(share * SUB, cols) for b in blocks], axis=0)


def series_kernel(w_ref, *refs):
    blocks, out_ref = refs[:-1], refs[-1]
    epochs, rows, cols = out_ref.shape
    deep = len(blocks) * blocks[0].shape[0] * SUB
    for t in range(rows // SUB):
        part = slice(t * SUB, (t + 1) * SUB)
        stack = stacked(blocks, part)
        for e in range(0, epochs, CUT):
            found = jnp.dot(w_ref[e * SUB : (e + CUT) * SUB, :deep], stack, preferred_element_type=F32)
            out_ref[e : e + CUT, part, :] = found.reshape(CUT, SUB, cols)


def displacement_kernel(w_ref, series_ref, *refs):
    blocks, (out_ref, held_ref, sem) = refs[:-3], refs[-3:]
    epochs, rows, cols = held_ref.shape
    deep = len(blocks) * blocks[0].shape[0] * SUB
    start = w_ref.shape[1] - deep
    parts = [slice(t * SUB, (t + 1) * SUB) for t in range(rows // SUB)]
    stacks = [stacked(blocks, part) for part in parts]
    copies = []
    for n, e in enumerate(range(0, epochs, CUT)):
        for part, stack in zip(parts, stacks):
            found = jnp.dot(w_ref[e * SUB : (e + CUT) * SUB, start:], stack, preferred_element_type=F32)
            found = found.reshape(CUT, SUB, cols) + series_ref[e : e + CUT, part, :]
            held_ref[e : e + CUT, part, :] = found.astype(BF16)
        copies.append(pltpu.make_async_copy(held_ref.at[e : e + CUT], out_ref.at[e : e + CUT], sem.at[n]))
        copies[-1].start()
    for copy in copies:
        copy.wait()


def banded(shape, axis, start):
    step = lax.broadcasted_iota(jnp.int32, shape, axis) - start
    step = step - lax.broadcasted_iota(jnp.int32, shape, 1 - axis)
    return jnp.where(jnp.abs(step) <= REACH, step, 0).astype(F32).astype(BF16)


def gradient_kernel(v_ref, right_ref, two_ref, left_ref, one_ref, rows_ref, cols_ref):
    rows, cols = v_ref.shape
    scale = (REACH * (REACH + 1) * (2 * REACH + 1) // 3) ** -0.5
    tile = lax.axis_index("grp") * lax.axis_size("row") + lax.axis_index("row")
    tiles = lax.axis_size("grp") * lax.axis_size("row")
    place, columns = lax.axis_index("col"), lax.axis_size("col")
    core, column = tile & 1, place & 1
    v = v_ref[...]
    one, two = one_ref[...], two_ref[...]
    above = jnp.where(tile == 0, 0.0, jnp.where(core == 0, two, one))
    below = jnp.where(tile == tiles - 1, 0.0, jnp.where(core == 0, one, two))
    upright = jnp.concatenate([above, v, below], axis=0)
    taps = banded((rows, rows + 2 * REACH), 1, REACH)
    total = jnp.zeros((rows, cols), F32)
    for part in three_parts(upright):
        total = total + jnp.dot(taps, part, preferred_element_type=F32)
    rows_ref[...] = total * scale
    first, second = left_ref[...], right_ref[...]
    before = jnp.where(place == 0, 0.0, jnp.where(column == 0, second, first))
    after = jnp.where(place == columns - 1, 0.0, jnp.where(column == 0, first, second))
    sideways = jnp.concatenate([before, v, after], axis=1)
    parts = jnp.concatenate(three_parts(sideways), axis=0)
    taps = banded((3 * LANES, LANES), 0, LANES)
    for c in range(0, cols, LANES):
        found = jnp.dot(parts[:, c : c + 3 * LANES], taps, preferred_element_type=F32)
        found = found[:rows] + found[rows : 2 * rows] + found[2 * rows :]
        cols_ref[:, c : c + LANES] = found * scale


VMEM = pl.BlockSpec(memory_space=pltpu.VMEM)


def call(kernel, inputs, outputs, flops, moved, limit=VMEM_BYTES, **more):
    return pl.pallas_call(
        kernel,
        in_specs=inputs,
        out_shape=outputs,
        cost_estimate=pl.CostEstimate(flops=flops, bytes_accessed=moved, transcendentals=0),
        compiler_params=pltpu.CompilerParams(vmem_limit_bytes=limit),
        **more,
    )


def shape(*dims, dtype=F32):
    return jax.ShapeDtypeStruct(dims, dtype)


def on_device(phase, pseudo_inverse, rotation, plate_id, coherent):
    share, groups, rows, cols = phase.shape
    epochs, ifg = pseudo_inverse.shape
    tiles = groups * lax.axis_size("row")
    both = ("grp", "row")
    tall, deep = epochs * SUB, ifg * SUB
    x, y, core = place_here()
    def cut(name):
        return lax.dynamic_index_in_dim(phase, partner(name, x, y, core, jnp.where), 1, keepdims=False)

    sent = {name: cut(name) for name in STARTS}
    got = {name: lax.ppermute(sent[name], both, swap_pairs(name)) for name in STARTS}
    later = (got[STARTS[0]], phase, pseudo_inverse, rotation, plate_id, coherent)
    got[STARTS[0]], phase, pseudo_inverse, rotation, plate_id, coherent = lax.optimization_barrier(later)
    early = [cut("own")] + [got[name] for name in EARLY]
    late = [got[name] for name in LATE]

    w, plate_rate, weight = call(
        prep_kernel,
        [VMEM, VMEM, VMEM],
        (shape(tall, deep, dtype=BF16), shape(rows, cols), shape(ifg, LANES)),
        2 * tall * deep * ifg,
        2 * tall * deep,
    )(rotation, pseudo_inverse, plate_id)

    series = call(
        series_kernel,
        [VMEM] * (1 + len(early)),
        shape(epochs, rows, cols),
        2 * epochs * ifg * rows * cols * SUB,
        2 * ifg * rows * cols,
    )(w, *early)
    series, plate_rate = lax.optimization_barrier((series, plate_rate))

    velocity, one, two, left, right = call(
        rate_kernel,
        [VMEM] * (3 + len(ORDER)),
        (shape(rows, cols), shape(REACH, cols), shape(REACH, cols), shape(rows, LANES), shape(rows, LANES)),
        2 * ifg * rows * cols,
        2 * ifg * rows * cols,
    )(weight, *early, *late, coherent, plate_rate)

    right = lax.ppermute(right, "col", ring_pairs(lax.axis_size("col"), 1))
    two = lax.ppermute(two, both, ring_pairs(tiles, 1))
    left = lax.ppermute(left, "col", ring_pairs(lax.axis_size("col"), 0))
    one = lax.ppermute(one, both, ring_pairs(tiles, 0))

    displacement = call(
        displacement_kernel,
        [VMEM] * (2 + len(late)),
        shape(epochs, rows, cols, dtype=BF16),
        epochs * ifg * rows * cols * SUB,
        2 * epochs * rows * cols,
        out_specs=pl.BlockSpec(memory_space=pl.ANY),
        scratch_shapes=[
            pltpu.VMEM((epochs, rows, cols), BF16),
            pltpu.SemaphoreType.DMA((epochs // CUT,)),
        ],
    )(w, series, *late)

    grad_rows, grad_cols = call(
        gradient_kernel,
        [VMEM] * 5,
        (shape(rows, cols), shape(rows, cols)),
        2 * 200 * rows * cols,
        16 * rows * cols,
    )(velocity, right, two, left, one)
    return (displacement, grad_rows, grad_cols)


def solution(mesh):
    return jax.shard_map(
        on_device,
        mesh=mesh,
        in_specs=(
            P("grp", None, "row", "col"),
            P(),
            P(),
            P(("grp", "row"), "col"),
            P(("grp", "row"), "col"),
        ),
        out_specs=(
            P(None, ("grp", "row"), "col"),
            P(("grp", "row"), "col"),
            P(("grp", "row"), "col"),
        ),
        check_vma=False,
    )
```

```python
import math

import jax
import jax.numpy as jnp
from jax import lax
from jax.experimental import pallas as pl
from jax.experimental.pallas import tpu as pltpu
from jax.sharding import PartitionSpec as P

REACH = 16
SUB = 16
LANES = 128
F32 = jnp.float32
BF16 = jnp.bfloat16
VMEM_BYTES = 40 << 20
WIDE = 72
CUT = 16

FLOWS = {
    "own": (0, 0),
    "D2": (2, 1),
    "Da": ("a", 1),
    "Db": ("b", 1),
    "X2": (2, 0),
    "Y2": (0, 1),
    "Xa": ("a", 0),
    "Xb": ("b", 0),
}
EARLY = ("D2", "Db", "X2", "Xa")
LATE = ("Y2", "Da", "Xb")
ORDER = ("own",) + EARLY + LATE
STARTS = ("D2", "Db", "X2", "Y2", "Da", "Xa", "Xb")


def along_x(step, x, core, pick):
    if step == "a":
        return pick(((x + core) & 1) == 0, 1, 3)
    if step == "b":
        return pick(((x + core) & 1) == 0, 3, 1)
    return step


def partner(flow, x, y, core, pick):
    step, turn = FLOWS[flow]
    return (((x + along_x(step, x, core, pick)) & 3) << 1) + ((y + turn) & 1)


def swap_pairs(flow):
    def choose(test, first, second):
        return first if test else second

    pairs = []
    for grp in range(8):
        for row in range(4):
            other = partner(flow, grp // 2, grp % 2, row % 2, choose)
            pairs.append((grp * 4 + row, other * 4 + row))
    return pairs


def neighbour_pairs(tiles, columns, along, first):
    pairs = []
    for tile in range(tiles):
        for column in range(columns):
            count = (tiles, columns)[along]
            here = (tile, column)[along]
            other = here + 1 if here % 2 == first else here - 1
            if 0 <= other < count:
                there = (other, column) if along == 0 else (tile, other)
            else:
                there = (tile, column ^ 1) if along == 0 else (tile ^ 1, column)
            pairs.append((tile * columns + column, there[0] * columns + there[1]))
    return pairs


def three_parts(value):
    high = value.astype(BF16)
    rest = value - high.astype(F32)
    mid = rest.astype(BF16)
    low = (rest - mid.astype(F32)).astype(BF16)
    return high, mid, low


def rate_weights(pinv_ref, weight_ref):
    epochs, ifg = pinv_ref.shape
    steps = lax.broadcasted_iota(jnp.int32, (epochs, LANES), 0).astype(F32) - (epochs - 1) / 2.0
    slope = steps * (epochs * (epochs * epochs - 1) / 12.0) ** -0.5
    total = jnp.zeros((ifg, LANES), F32)
    for part in three_parts(slope):
        total = total + lax.dot_general(
            pinv_ref[...], part, (((0,), (0,)), ((), ())), preferred_element_type=F32
        )
    weight_ref[...] = total


def prep_kernel(rot_ref, pinv_ref, plate_ref, w_ref, rate_ref, weight_ref):
    rate_weights(pinv_ref, weight_ref)
    epochs, ifg = pinv_ref.shape
    rows, cols = plate_ref.shape
    x, y, core = place_here()
    tall = epochs * SUB
    grow = lax.broadcasted_iota(jnp.int32, (tall, epochs), 0) // SUB
    pick = (grow == lax.broadcasted_iota(jnp.int32, (tall, epochs), 1)).astype(BF16)
    tall_inverse = jnp.dot(pick, pinv_ref[...], preferred_element_type=F32).astype(BF16)
    share = ifg // 8
    wide = share * SUB
    here = lax.broadcasted_iota(jnp.int32, (ifg, wide), 0)
    there = lax.broadcasted_iota(jnp.int32, (ifg, wide), 1) // SUB
    diagonal = (lax.broadcasted_iota(jnp.int32, (tall, wide), 0) % SUB) == (
        lax.broadcasted_iota(jnp.int32, (tall, wide), 1) % SUB
    )
    for k, name in enumerate(ORDER):
        source = partner(name, x, y, core, jnp.where)
        spread = (here == there + source * share).astype(BF16)
        block = jnp.dot(tall_inverse, spread, preferred_element_type=F32)
        w_ref[:, k * wide : (k + 1) * wide] = jnp.where(diagonal, block, 0.0).astype(BF16)
    tile = lax.axis_index("grp") * lax.axis_size("row") + lax.axis_index("row")
    total_rows = rows * lax.axis_size("grp") * lax.axis_size("row")
    total_cols = cols * lax.axis_size("col")
    down = lax.broadcasted_iota(jnp.int32, (rows, LANES), 0) + tile * rows
    over = lax.broadcasted_iota(jnp.int32, (8, cols), 1) + lax.axis_index("col") * cols
    lat = (36.0 + 6.0 * (down.astype(F32) + 0.5) / total_rows) * (math.pi / 180.0)
    lon = (26.0 + 19.0 * (over.astype(F32) + 0.5) / total_cols) * (math.pi / 180.0)
    cos_lat, sin_lat = jnp.cos(lat)[:, 0:1], jnp.sin(lat)[:, 0:1]
    cos_lon, sin_lon = jnp.cos(lon)[0:1, :], jnp.sin(lon)[0:1, :]
    sx, sy, sz = (0.38, -0.08, 0.92)
    px = cos_lat * cos_lon
    py = cos_lat * sin_lon
    pz = sin_lat + 0.0 * sin_lon
    lever = (py * sz - pz * sy, pz * sx - px * sz, px * sy - py * sx)
    plate = plate_ref[...]
    total = jnp.zeros(plate.shape, F32)
    for p in range(rot_ref.shape[0]):
        along = jnp.zeros(plate.shape, F32)
        for k in range(3):
            along = along + rot_ref[p : p + 1, k : k + 1] * lever[k]
        total = total + jnp.where(plate == p, along, 0.0)
    rate_ref[...] = total


def weighted(total, block, weight_ref, source):
    share, _, cols = block.shape
    for i in range(share):
        row = weight_ref[pl.ds(source * share + i, 1), :]
        total = total + jnp.concatenate([row] * (cols // LANES), axis=1) * block[i].astype(F32)
    return total


def place_here():
    grp, row = lax.axis_index("grp"), lax.axis_index("row")
    return grp >> 1, grp & 1, row & 1


def rates(total, weight_ref, names, blocks):
    x, y, core = place_here()
    for name, block in zip(names, blocks):
        total = weighted(total, block, weight_ref, partner(name, x, y, core, jnp.where))
    return total


def rate_kernel(weight_ref, part_ref, *refs):
    v_ref, one_ref, two_ref, left_ref, right_ref = refs[-5:]
    coherent_ref, plate_rate_ref = refs[-7:-5]
    rows, cols = v_ref.shape
    rate = rates(part_ref[...], weight_ref, LATE, refs[:-7])
    v_ref[...] = coherent_ref[...].astype(F32) * rate - plate_rate_ref[...]
    core = place_here()[2]
    column = lax.axis_index("col") & 1
    top, low = v_ref[:REACH, :], v_ref[rows - REACH :, :]
    first, last = v_ref[:, :LANES], v_ref[:, cols - LANES :]
    one_ref[...] = jnp.where(core == 0, low, top)
    two_ref[...] = jnp.where(core == 0, top, low)
    left_ref[...] = jnp.where(column == 0, last, first)
    right_ref[:rows, :] = jnp.where(column == 0, first, last)
    right_ref[rows:, :] = jnp.zeros((WIDE - rows, LANES), F32)


def stacked(blocks, part):
    share, _, cols = blocks[0].shape
    return jnp.concatenate([b[:, part, :].reshape(share * SUB, cols) for b in blocks], axis=0)


def series_kernel(w_ref, weight_ref, *refs):
    blocks, out_ref, rate_ref = refs[:-2], refs[-2], refs[-1]
    epochs, rows, cols = out_ref.shape
    deep = len(blocks) * blocks[0].shape[0] * SUB
    for t in range(rows // SUB):
        part = slice(t * SUB, (t + 1) * SUB)
        stack = stacked(blocks, part)
        for e in range(0, epochs, CUT):
            found = jnp.dot(w_ref[e * SUB : (e + CUT) * SUB, :deep], stack, preferred_element_type=F32)
            out_ref[e : e + CUT, part, :] = found.reshape(CUT, SUB, cols)
    rate_ref[...] = rates(jnp.zeros((rows, cols), F32), weight_ref, ("own",) + EARLY, blocks)


def displacement_kernel(w_ref, series_ref, *refs):
    blocks, (out_ref, held_ref, sem) = refs[:-3], refs[-3:]
    epochs, rows, cols = held_ref.shape
    deep = len(blocks) * blocks[0].shape[0] * SUB
    start = w_ref.shape[1] - deep
    parts = [slice(t * SUB, (t + 1) * SUB) for t in range(rows // SUB)]
    stacks = [stacked(blocks, part) for part in parts]
    copies = []
    for n, e in enumerate(range(0, epochs, CUT)):
        for part, stack in zip(parts, stacks):
            found = jnp.dot(w_ref[e * SUB : (e + CUT) * SUB, start:], stack, preferred_element_type=F32)
            found = found.reshape(CUT, SUB, cols) + series_ref[e : e + CUT, part, :]
            held_ref[e : e + CUT, part, :] = found.astype(BF16)
        copies.append(pltpu.make_async_copy(held_ref.at[e : e + CUT], out_ref.at[e : e + CUT], sem.at[n]))
        copies[-1].start()
    for copy in copies:
        copy.wait()


def banded(shape, axis, start):
    step = lax.broadcasted_iota(jnp.int32, shape, axis) - start
    step = step - lax.broadcasted_iota(jnp.int32, shape, 1 - axis)
    return jnp.where(jnp.abs(step) <= REACH, step, 0).astype(F32).astype(BF16)


def gradient_kernel(v_ref, right_ref, two_ref, one_ref, left_ref, rows_ref, cols_ref):
    rows, cols = v_ref.shape
    scale = (REACH * (REACH + 1) * (2 * REACH + 1) // 3) ** -0.5
    tile = lax.axis_index("grp") * lax.axis_size("row") + lax.axis_index("row")
    tiles = lax.axis_size("grp") * lax.axis_size("row")
    place, columns = lax.axis_index("col"), lax.axis_size("col")
    core, column = tile & 1, place & 1
    v = v_ref[...]
    one, two = one_ref[...], two_ref[...]
    above = jnp.where(tile == 0, 0.0, jnp.where(core == 0, two, one))
    below = jnp.where(tile == tiles - 1, 0.0, jnp.where(core == 0, one, two))
    upright = jnp.concatenate([above, v, below], axis=0)
    taps = banded((rows, rows + 2 * REACH), 1, REACH)
    total = jnp.zeros((rows, cols), F32)
    for part in three_parts(upright):
        total = total + jnp.dot(taps, part, preferred_element_type=F32)
    rows_ref[...] = total * scale
    first, second = left_ref[...], right_ref[:rows, :]
    before = jnp.where(place == 0, 0.0, jnp.where(column == 0, second, first))
    after = jnp.where(place == columns - 1, 0.0, jnp.where(column == 0, first, second))
    sideways = jnp.concatenate([before, v, after], axis=1)
    parts = jnp.concatenate(three_parts(sideways), axis=0)
    taps = banded((3 * LANES, LANES), 0, LANES)
    for c in range(0, cols, LANES):
        found = jnp.dot(parts[:, c : c + 3 * LANES], taps, preferred_element_type=F32)
        found = found[:rows] + found[rows : 2 * rows] + found[2 * rows :]
        cols_ref[:, c : c + LANES] = found * scale


VMEM = pl.BlockSpec(memory_space=pltpu.VMEM)


def call(kernel, inputs, outputs, flops, moved, limit=VMEM_BYTES, **more):
    return pl.pallas_call(
        kernel,
        in_specs=inputs,
        out_shape=outputs,
        cost_estimate=pl.CostEstimate(flops=flops, bytes_accessed=moved, transcendentals=0),
        compiler_params=pltpu.CompilerParams(vmem_limit_bytes=limit),
        **more,
    )


def shape(*dims, dtype=F32):
    return jax.ShapeDtypeStruct(dims, dtype)


def on_device(phase, pseudo_inverse, rotation, plate_id, coherent):
    share, groups, rows, cols = phase.shape
    epochs, ifg = pseudo_inverse.shape
    tiles = groups * lax.axis_size("row")
    both = ("grp", "row")
    tall, deep = epochs * SUB, ifg * SUB
    x, y, core = place_here()
    def cut(name):
        return lax.dynamic_index_in_dim(phase, partner(name, x, y, core, jnp.where), 1, keepdims=False)

    sent = {name: cut(name) for name in STARTS}
    got = {name: lax.ppermute(sent[name], both, swap_pairs(name)) for name in STARTS}
    later = (got[STARTS[0]], phase, pseudo_inverse, rotation, plate_id, coherent)
    got[STARTS[0]], phase, pseudo_inverse, rotation, plate_id, coherent = lax.optimization_barrier(later)
    early = [cut("own")] + [got[name] for name in EARLY]
    late = [got[name] for name in LATE]

    w, plate_rate, weight = call(
        prep_kernel,
        [VMEM, VMEM, VMEM],
        (shape(tall, deep, dtype=BF16), shape(rows, cols), shape(ifg, LANES)),
        2 * tall * deep * ifg,
        2 * tall * deep,
    )(rotation, pseudo_inverse, plate_id)

    series, rate = call(
        series_kernel,
        [VMEM] * (2 + len(early)),
        (shape(epochs, rows, cols), shape(rows, cols)),
        2 * epochs * ifg * rows * cols * SUB,
        2 * ifg * rows * cols,
    )(w, weight, *early)
    series, plate_rate = lax.optimization_barrier((series, plate_rate))

    velocity, one, two, left, right = call(
        rate_kernel,
        [VMEM] * (4 + len(late)),
        (shape(rows, cols), shape(REACH, cols), shape(REACH, cols), shape(rows, LANES), shape(WIDE, LANES)),
        2 * ifg * rows * cols,
        2 * ifg * rows * cols,
    )(weight, rate, *late, coherent, plate_rate)

    columns = lax.axis_size("col")
    everywhere = ("grp", "row", "col")
    right = lax.ppermute(right, everywhere, neighbour_pairs(tiles, columns, 1, 1))
    one = lax.ppermute(one, everywhere, neighbour_pairs(tiles, columns, 0, 0))
    two = lax.ppermute(two, everywhere, neighbour_pairs(tiles, columns, 0, 1))
    left = lax.ppermute(left, everywhere, neighbour_pairs(tiles, columns, 1, 0))
    displacement = call(
        displacement_kernel,
        [VMEM] * (2 + len(late)),
        shape(epochs, rows, cols, dtype=BF16),
        epochs * ifg * rows * cols * SUB,
        2 * epochs * rows * cols,
        out_specs=pl.BlockSpec(memory_space=pl.ANY),
        scratch_shapes=[
            pltpu.VMEM((epochs, rows, cols), BF16),
            pltpu.SemaphoreType.DMA((epochs // CUT,)),
        ],
    )(w, series, *late)

    grad_rows, grad_cols = call(
        gradient_kernel,
        [VMEM] * 5,
        (shape(rows, cols), shape(rows, cols)),
        2 * 200 * rows * cols,
        16 * rows * cols,
    )(velocity, right, two, one, left)
    return (displacement, grad_rows, grad_cols)


def solution(mesh):
    return jax.shard_map(
        on_device,
        mesh=mesh,
        in_specs=(
            P("grp", None, "row", "col"),
            P(),
            P(),
            P(("grp", "row"), "col"),
            P(("grp", "row"), "col"),
        ),
        out_specs=(
            P(None, ("grp", "row"), "col"),
            P(("grp", "row"), "col"),
            P(("grp", "row"), "col"),
        ),
        check_vma=False,
    )
```

```python
import math

import jax
import jax.numpy as jnp
from jax import lax
from jax.experimental import pallas as pl
from jax.experimental.pallas import tpu as pltpu
from jax.sharding import PartitionSpec as P

REACH = 16
SUB = 16
LANES = 128
F32 = jnp.float32
BF16 = jnp.bfloat16
VMEM_BYTES = 40 << 20
EXTRA = 8
CUT = 16

FLOWS = {
    "own": (0, 0),
    "D2": (2, 1),
    "Da": ("a", 1),
    "Db": ("b", 1),
    "X2": (2, 0),
    "Y2": (0, 1),
    "Xa": ("a", 0),
    "Xb": ("b", 0),
}
EARLY = ("D2", "Xa", "Db", "X2")
LATE = ("Da", "Y2", "Xb")
ORDER = ("own",) + EARLY + LATE
STARTS = EARLY + LATE


def along_x(step, x, core, pick):
    if step == "a":
        return pick(((x + core) & 1) == 0, 1, 3)
    if step == "b":
        return pick(((x + core) & 1) == 0, 3, 1)
    return step


def partner(flow, x, y, core, pick):
    step, turn = FLOWS[flow]
    return (((x + along_x(step, x, core, pick)) & 3) << 1) + ((y + turn) & 1)


def swap_pairs(flow):
    def choose(test, first, second):
        return first if test else second

    pairs = []
    for grp in range(8):
        for row in range(4):
            other = partner(flow, grp // 2, grp % 2, row % 2, choose)
            pairs.append((grp * 4 + row, other * 4 + row))
    return pairs


def neighbour_pairs(tiles, columns, along, first):
    pairs = []
    for tile in range(tiles):
        for column in range(columns):
            count = (tiles, columns)[along]
            here = (tile, column)[along]
            other = here + 1 if here % 2 == first else here - 1
            if 0 <= other < count:
                there = (other, column) if along == 0 else (tile, other)
            else:
                there = (tile, column ^ 1) if along == 0 else (tile ^ 1, column)
            pairs.append((tile * columns + column, there[0] * columns + there[1]))
    return pairs


def three_parts(value):
    high = value.astype(BF16)
    rest = value - high.astype(F32)
    mid = rest.astype(BF16)
    low = (rest - mid.astype(F32)).astype(BF16)
    return high, mid, low


def rate_weights(pinv_ref, weight_ref):
    epochs, ifg = pinv_ref.shape
    steps = lax.broadcasted_iota(jnp.int32, (epochs, LANES), 0).astype(F32) - (epochs - 1) / 2.0
    slope = steps * (epochs * (epochs * epochs - 1) / 12.0) ** -0.5
    total = jnp.zeros((ifg, LANES), F32)
    for part in three_parts(slope):
        total = total + lax.dot_general(
            pinv_ref[...], part, (((0,), (0,)), ((), ())), preferred_element_type=F32
        )
    weight_ref[...] = total


def prep_kernel(rot_ref, pinv_ref, plate_ref, w_ref, rate_ref, weight_ref):
    rate_weights(pinv_ref, weight_ref)
    epochs, ifg = pinv_ref.shape
    rows, cols = plate_ref.shape
    x, y, core = place_here()
    tall = epochs * SUB
    grow = lax.broadcasted_iota(jnp.int32, (tall, epochs), 0) // SUB
    pick = (grow == lax.broadcasted_iota(jnp.int32, (tall, epochs), 1)).astype(BF16)
    tall_inverse = jnp.dot(pick, pinv_ref[...], preferred_element_type=F32).astype(BF16)
    share = ifg // 8
    wide = share * SUB
    here = lax.broadcasted_iota(jnp.int32, (ifg, wide), 0)
    there = lax.broadcasted_iota(jnp.int32, (ifg, wide), 1) // SUB
    diagonal = (lax.broadcasted_iota(jnp.int32, (tall, wide), 0) % SUB) == (
        lax.broadcasted_iota(jnp.int32, (tall, wide), 1) % SUB
    )
    for k, name in enumerate(ORDER):
        source = partner(name, x, y, core, jnp.where)
        spread = (here == there + source * share).astype(BF16)
        block = jnp.dot(tall_inverse, spread, preferred_element_type=F32)
        w_ref[:, k * wide : (k + 1) * wide] = jnp.where(diagonal, block, 0.0).astype(BF16)
    tile = lax.axis_index("grp") * lax.axis_size("row") + lax.axis_index("row")
    total_rows = rows * lax.axis_size("grp") * lax.axis_size("row")
    total_cols = cols * lax.axis_size("col")
    down = lax.broadcasted_iota(jnp.int32, (rows, LANES), 0) + tile * rows
    over = lax.broadcasted_iota(jnp.int32, (8, cols), 1) + lax.axis_index("col") * cols
    lat = (36.0 + 6.0 * (down.astype(F32) + 0.5) / total_rows) * (math.pi / 180.0)
    lon = (26.0 + 19.0 * (over.astype(F32) + 0.5) / total_cols) * (math.pi / 180.0)
    cos_lat, sin_lat = jnp.cos(lat)[:, 0:1], jnp.sin(lat)[:, 0:1]
    cos_lon, sin_lon = jnp.cos(lon)[0:1, :], jnp.sin(lon)[0:1, :]
    sx, sy, sz = (0.38, -0.08, 0.92)
    px = cos_lat * cos_lon
    py = cos_lat * sin_lon
    pz = sin_lat + 0.0 * sin_lon
    lever = (py * sz - pz * sy, pz * sx - px * sz, px * sy - py * sx)
    plate = plate_ref[...]
    total = jnp.zeros(plate.shape, F32)
    for p in range(rot_ref.shape[0]):
        along = jnp.zeros(plate.shape, F32)
        for k in range(3):
            along = along + rot_ref[p : p + 1, k : k + 1] * lever[k]
        total = total + jnp.where(plate == p, along, 0.0)
    rate_ref[...] = total


def weighted(total, block, weight_ref, source):
    share, _, cols = block.shape
    for i in range(share):
        row = weight_ref[pl.ds(source * share + i, 1), :]
        total = total + jnp.concatenate([row] * (cols // LANES), axis=1) * block[i].astype(F32)
    return total


def place_here():
    grp, row = lax.axis_index("grp"), lax.axis_index("row")
    return grp >> 1, grp & 1, row & 1


def rates(total, weight_ref, names, blocks):
    x, y, core = place_here()
    for name, block in zip(names, blocks):
        total = weighted(total, block, weight_ref, partner(name, x, y, core, jnp.where))
    return total


def rate_kernel(weight_ref, part_ref, *refs):
    v_ref, one_ref, two_ref, left_ref, right_ref = refs[-5:]
    coherent_ref, plate_rate_ref = refs[-7:-5]
    rows, cols = v_ref.shape
    rate = rates(part_ref[...], weight_ref, LATE, refs[:-7])
    v_ref[...] = coherent_ref[...].astype(F32) * rate - plate_rate_ref[...]
    core = place_here()[2]
    column = lax.axis_index("col") & 1
    top, low = v_ref[:REACH, :], v_ref[rows - REACH :, :]
    first, last = v_ref[:, :LANES], v_ref[:, cols - LANES :]
    one_ref[...] = jnp.where(core == 0, low, top)
    two_ref[...] = jnp.where(core == 0, top, low)
    left_ref[:rows, :] = jnp.where(column == 0, last, first)
    left_ref[rows:, :] = jnp.zeros((EXTRA, LANES), F32)
    right_ref[:rows, :] = jnp.where(column == 0, first, last)


def stacked(blocks, part):
    share, _, cols = blocks[0].shape
    return jnp.concatenate([b[:, part, :].reshape(share * SUB, cols) for b in blocks], axis=0)


def series_kernel(w_ref, weight_ref, *refs):
    blocks, out_ref, rate_ref = refs[:-2], refs[-2], refs[-1]
    epochs, rows, cols = out_ref.shape
    deep = len(blocks) * blocks[0].shape[0] * SUB
    for t in range(rows // SUB):
        part = slice(t * SUB, (t + 1) * SUB)
        stack = stacked(blocks, part)
        for e in range(0, epochs, CUT):
            found = jnp.dot(w_ref[e * SUB : (e + CUT) * SUB, :deep], stack, preferred_element_type=F32)
            out_ref[e : e + CUT, part, :] = found.reshape(CUT, SUB, cols)
    rate_ref[...] = rates(jnp.zeros((rows, cols), F32), weight_ref, ("own",) + EARLY, blocks)


def displacement_kernel(w_ref, series_ref, *refs):
    blocks, (out_ref, held_ref, sem) = refs[:-3], refs[-3:]
    epochs, rows, cols = held_ref.shape
    deep = len(blocks) * blocks[0].shape[0] * SUB
    start = w_ref.shape[1] - deep
    parts = [slice(t * SUB, (t + 1) * SUB) for t in range(rows // SUB)]
    stacks = [stacked(blocks, part) for part in parts]
    copies = []
    for n, e in enumerate(range(0, epochs, CUT)):
        for part, stack in zip(parts, stacks):
            found = jnp.dot(w_ref[e * SUB : (e + CUT) * SUB, start:], stack, preferred_element_type=F32)
            found = found.reshape(CUT, SUB, cols) + series_ref[e : e + CUT, part, :]
            held_ref[e : e + CUT, part, :] = found.astype(BF16)
        copies.append(pltpu.make_async_copy(held_ref.at[e : e + CUT], out_ref.at[e : e + CUT], sem.at[n]))
        copies[-1].start()
    for copy in copies:
        copy.wait()


def banded(shape, axis, start):
    step = lax.broadcasted_iota(jnp.int32, shape, axis) - start
    step = step - lax.broadcasted_iota(jnp.int32, shape, 1 - axis)
    return jnp.where(jnp.abs(step) <= REACH, step, 0).astype(F32).astype(BF16)


def gradient_kernel(v_ref, right_ref, two_ref, one_ref, left_ref, rows_ref, cols_ref):
    rows, cols = v_ref.shape
    scale = (REACH * (REACH + 1) * (2 * REACH + 1) // 3) ** -0.5
    tile = lax.axis_index("grp") * lax.axis_size("row") + lax.axis_index("row")
    tiles = lax.axis_size("grp") * lax.axis_size("row")
    place, columns = lax.axis_index("col"), lax.axis_size("col")
    core, column = tile & 1, place & 1
    v = v_ref[...]
    one, two = one_ref[...], two_ref[...]
    above = jnp.where(tile == 0, 0.0, jnp.where(core == 0, two, one))
    below = jnp.where(tile == tiles - 1, 0.0, jnp.where(core == 0, one, two))
    upright = jnp.concatenate([above, v, below], axis=0)
    taps = banded((rows, rows + 2 * REACH), 1, REACH)
    total = jnp.zeros((rows, cols), F32)
    for part in three_parts(upright):
        total = total + jnp.dot(taps, part, preferred_element_type=F32)
    rows_ref[...] = total * scale
    first, second = left_ref[:rows, :], right_ref[:rows, :]
    before = jnp.where(place == 0, 0.0, jnp.where(column == 0, second, first))
    after = jnp.where(place == columns - 1, 0.0, jnp.where(column == 0, first, second))
    sideways = jnp.concatenate([before, v, after], axis=1)
    parts = jnp.concatenate(three_parts(sideways), axis=0)
    taps = banded((3 * LANES, LANES), 0, LANES)
    for c in range(0, cols, LANES):
        found = jnp.dot(parts[:, c : c + 3 * LANES], taps, preferred_element_type=F32)
        found = found[:rows] + found[rows : 2 * rows] + found[2 * rows :]
        cols_ref[:, c : c + LANES] = found * scale


VMEM = pl.BlockSpec(memory_space=pltpu.VMEM)


def call(kernel, inputs, outputs, flops, moved, limit=VMEM_BYTES, **more):
    return pl.pallas_call(
        kernel,
        in_specs=inputs,
        out_shape=outputs,
        cost_estimate=pl.CostEstimate(flops=flops, bytes_accessed=moved, transcendentals=0),
        compiler_params=pltpu.CompilerParams(vmem_limit_bytes=limit),
        **more,
    )


def shape(*dims, dtype=F32):
    return jax.ShapeDtypeStruct(dims, dtype)


def on_device(phase, pseudo_inverse, rotation, plate_id, coherent):
    share, groups, rows, cols = phase.shape
    epochs, ifg = pseudo_inverse.shape
    tiles = groups * lax.axis_size("row")
    both = ("grp", "row")
    tall, deep = epochs * SUB, ifg * SUB
    x, y, core = place_here()
    def cut(name):
        return lax.dynamic_index_in_dim(phase, partner(name, x, y, core, jnp.where), 1, keepdims=False)

    sent = {name: cut(name) for name in STARTS}
    got = {name: lax.ppermute(sent[name], both, swap_pairs(name)) for name in STARTS}
    later = (got[STARTS[0]], phase, pseudo_inverse, rotation, plate_id, coherent)
    got[STARTS[0]], phase, pseudo_inverse, rotation, plate_id, coherent = lax.optimization_barrier(later)
    early = [cut("own")] + [got[name] for name in EARLY]
    late = [got[name] for name in LATE]

    w, plate_rate, weight = call(
        prep_kernel,
        [VMEM, VMEM, VMEM],
        (shape(tall, deep, dtype=BF16), shape(rows, cols), shape(ifg, LANES)),
        2 * tall * deep * ifg,
        2 * tall * deep,
    )(rotation, pseudo_inverse, plate_id)

    series, rate = call(
        series_kernel,
        [VMEM] * (2 + len(early)),
        (shape(epochs, rows, cols), shape(rows, cols)),
        2 * epochs * ifg * rows * cols * SUB,
        2 * ifg * rows * cols,
    )(w, weight, *early)
    series, plate_rate = lax.optimization_barrier((series, plate_rate))

    velocity, one, two, left, right = call(
        rate_kernel,
        [VMEM] * (4 + len(late)),
        (shape(rows, cols), shape(REACH, cols), shape(REACH, cols), shape(rows + EXTRA, LANES), shape(rows, LANES)),
        2 * ifg * rows * cols,
        2 * ifg * rows * cols,
    )(weight, rate, *late, coherent, plate_rate)

    columns = lax.axis_size("col")
    everywhere = ("grp", "row", "col")
    right = lax.ppermute(right, everywhere, neighbour_pairs(tiles, columns, 1, 1))
    one = lax.ppermute(one, everywhere, neighbour_pairs(tiles, columns, 0, 0))
    two = lax.ppermute(two, everywhere, neighbour_pairs(tiles, columns, 0, 1))
    left = lax.ppermute(left, everywhere, neighbour_pairs(tiles, columns, 1, 0))
    displacement = call(
        displacement_kernel,
        [VMEM] * (2 + len(late)),
        shape(epochs, rows, cols, dtype=BF16),
        epochs * ifg * rows * cols * SUB,
        2 * epochs * rows * cols,
        out_specs=pl.BlockSpec(memory_space=pl.ANY),
        scratch_shapes=[
            pltpu.VMEM((epochs, rows, cols), BF16),
            pltpu.SemaphoreType.DMA((epochs // CUT,)),
        ],
    )(w, series, *late)

    grad_rows, grad_cols = call(
        gradient_kernel,
        [VMEM] * 5,
        (shape(rows, cols), shape(rows, cols)),
        2 * 200 * rows * cols,
        16 * rows * cols,
    )(velocity, right, two, one, left)
    return (displacement, grad_rows, grad_cols)


def solution(mesh):
    return jax.shard_map(
        on_device,
        mesh=mesh,
        in_specs=(
            P("grp", None, "row", "col"),
            P(),
            P(),
            P(("grp", "row"), "col"),
            P(("grp", "row"), "col"),
        ),
        out_specs=(
            P(None, ("grp", "row"), "col"),
            P(("grp", "row"), "col"),
            P(("grp", "row"), "col"),
        ),
        check_vma=False,
    )
```

```python
import math

import jax
import jax.numpy as jnp
from jax import lax
from jax.experimental import pallas as pl
from jax.experimental.pallas import tpu as pltpu
from jax.sharding import PartitionSpec as P

REACH = 16
SUB = 16
LANES = 128
F32 = jnp.float32
BF16 = jnp.bfloat16
VMEM_BYTES = 40 << 20
EXTRA = 8
CUT = 16

FLOWS = {
    "own": (0, 0),
    "D2": (2, 1),
    "Da": ("a", 1),
    "Db": ("b", 1),
    "X2": (2, 0),
    "Y2": (0, 1),
    "Xa": ("a", 0),
    "Xb": ("b", 0),
}
EARLY = ("D2", "Xa", "Db", "X2")
LATE = ("Da", "Y2", "Xb")
ORDER = ("own",) + EARLY + LATE
STARTS = EARLY + LATE


def along_x(step, x, core, pick):
    if step == "a":
        return pick(((x + core) & 1) == 0, 1, 3)
    if step == "b":
        return pick(((x + core) & 1) == 0, 3, 1)
    return step


def partner(flow, x, y, core, pick):
    step, turn = FLOWS[flow]
    return (((x + along_x(step, x, core, pick)) & 3) << 1) + ((y + turn) & 1)


def swap_pairs(flow):
    def choose(test, first, second):
        return first if test else second

    pairs = []
    for grp in range(8):
        for row in range(4):
            other = partner(flow, grp // 2, grp % 2, row % 2, choose)
            pairs.append((grp * 4 + row, other * 4 + row))
    return pairs


def neighbour_pairs(tiles, columns, along, first):
    pairs = []
    for tile in range(tiles):
        for column in range(columns):
            count = (tiles, columns)[along]
            here = (tile, column)[along]
            other = here + 1 if here % 2 == first else here - 1
            if 0 <= other < count:
                there = (other, column) if along == 0 else (tile, other)
            else:
                there = (tile, column ^ 1) if along == 0 else (tile ^ 1, column)
            pairs.append((tile * columns + column, there[0] * columns + there[1]))
    return pairs


def three_parts(value):
    high = value.astype(BF16)
    rest = value - high.astype(F32)
    mid = rest.astype(BF16)
    low = (rest - mid.astype(F32)).astype(BF16)
    return high, mid, low


def rate_weights(pinv_ref, weight_ref):
    epochs, ifg = pinv_ref.shape
    steps = lax.broadcasted_iota(jnp.int32, (epochs, LANES), 0).astype(F32) - (epochs - 1) / 2.0
    slope = steps * (epochs * (epochs * epochs - 1) / 12.0) ** -0.5
    total = jnp.zeros((ifg, LANES), F32)
    for part in three_parts(slope):
        total = total + lax.dot_general(
            pinv_ref[...], part, (((0,), (0,)), ((), ())), preferred_element_type=F32
        )
    weight_ref[...] = total


def prep_kernel(rot_ref, pinv_ref, plate_ref, w_ref, rate_ref, weight_ref):
    rate_weights(pinv_ref, weight_ref)
    epochs, ifg = pinv_ref.shape
    rows, cols = plate_ref.shape
    x, y, core = place_here()
    tall = epochs * SUB
    grow = lax.broadcasted_iota(jnp.int32, (tall, epochs), 0) // SUB
    pick = (grow == lax.broadcasted_iota(jnp.int32, (tall, epochs), 1)).astype(BF16)
    tall_inverse = jnp.dot(pick, pinv_ref[...], preferred_element_type=F32).astype(BF16)
    share = ifg // 8
    wide = share * SUB
    here = lax.broadcasted_iota(jnp.int32, (ifg, wide), 0)
    there = lax.broadcasted_iota(jnp.int32, (ifg, wide), 1) // SUB
    diagonal = (lax.broadcasted_iota(jnp.int32, (tall, wide), 0) % SUB) == (
        lax.broadcasted_iota(jnp.int32, (tall, wide), 1) % SUB
    )
    for k, name in enumerate(ORDER):
        source = partner(name, x, y, core, jnp.where)
        spread = (here == there + source * share).astype(BF16)
        block = jnp.dot(tall_inverse, spread, preferred_element_type=F32)
        w_ref[:, k * wide : (k + 1) * wide] = jnp.where(diagonal, block, 0.0).astype(BF16)
    tile = lax.axis_index("grp") * lax.axis_size("row") + lax.axis_index("row")
    total_rows = rows * lax.axis_size("grp") * lax.axis_size("row")
    total_cols = cols * lax.axis_size("col")
    down = lax.broadcasted_iota(jnp.int32, (rows, LANES), 0) + tile * rows
    over = lax.broadcasted_iota(jnp.int32, (8, cols), 1) + lax.axis_index("col") * cols
    lat = (36.0 + 6.0 * (down.astype(F32) + 0.5) / total_rows) * (math.pi / 180.0)
    lon = (26.0 + 19.0 * (over.astype(F32) + 0.5) / total_cols) * (math.pi / 180.0)
    cos_lat, sin_lat = jnp.cos(lat)[:, 0:1], jnp.sin(lat)[:, 0:1]
    cos_lon, sin_lon = jnp.cos(lon)[0:1, :], jnp.sin(lon)[0:1, :]
    sx, sy, sz = (0.38, -0.08, 0.92)
    px = cos_lat * cos_lon
    py = cos_lat * sin_lon
    pz = sin_lat + 0.0 * sin_lon
    lever = (py * sz - pz * sy, pz * sx - px * sz, px * sy - py * sx)
    plate = plate_ref[...]
    total = jnp.zeros(plate.shape, F32)
    for p in range(rot_ref.shape[0]):
        along = jnp.zeros(plate.shape, F32)
        for k in range(3):
            along = along + rot_ref[p : p + 1, k : k + 1] * lever[k]
        total = total + jnp.where(plate == p, along, 0.0)
    rate_ref[...] = total


def weighted(total, block, weight_ref, source):
    share, _, cols = block.shape
    for i in range(share):
        row = weight_ref[pl.ds(source * share + i, 1), :]
        total = total + jnp.concatenate([row] * (cols // LANES), axis=1) * block[i].astype(F32)
    return total


def place_here():
    grp, row = lax.axis_index("grp"), lax.axis_index("row")
    return grp >> 1, grp & 1, row & 1


def rates(total, weight_ref, names, blocks):
    x, y, core = place_here()
    for name, block in zip(names, blocks):
        total = weighted(total, block, weight_ref, partner(name, x, y, core, jnp.where))
    return total


def rate_kernel(weight_ref, part_ref, *refs):
    v_ref, one_ref, two_ref, left_ref, right_ref = refs[-5:]
    coherent_ref, plate_rate_ref = refs[-7:-5]
    rows, cols = v_ref.shape
    rate = rates(part_ref[...], weight_ref, LATE, refs[:-7])
    v_ref[...] = coherent_ref[...].astype(F32) * rate - plate_rate_ref[...]
    core = place_here()[2]
    column = lax.axis_index("col") & 1
    top, low = v_ref[:REACH, :], v_ref[rows - REACH :, :]
    first, last = v_ref[:, :LANES], v_ref[:, cols - LANES :]
    one_ref[...] = jnp.where(core == 0, low, top)
    two_ref[...] = jnp.where(core == 0, top, low)
    left_ref[:rows, :] = jnp.where(column == 0, last, first)
    left_ref[rows:, :] = jnp.zeros((EXTRA, LANES), F32)
    right_ref[:rows, :] = jnp.where(column == 0, first, last)


def stacked(blocks, part):
    share, _, cols = blocks[0].shape
    return jnp.concatenate([b[:, part, :].reshape(share * SUB, cols) for b in blocks], axis=0)


def series_kernel(w_ref, weight_ref, *refs):
    blocks, out_ref, rate_ref = refs[:-2], refs[-2], refs[-1]
    epochs, rows, cols = out_ref.shape
    deep = len(blocks) * blocks[0].shape[0] * SUB
    for t in range(rows // SUB):
        part = slice(t * SUB, (t + 1) * SUB)
        stack = stacked(blocks, part)
        for e in range(0, epochs, CUT):
            found = jnp.dot(w_ref[e * SUB : (e + CUT) * SUB, :deep], stack, preferred_element_type=F32)
            out_ref[e : e + CUT, part, :] = found.reshape(CUT, SUB, cols)
    rate_ref[...] = rates(jnp.zeros((rows, cols), F32), weight_ref, ("own",) + EARLY, blocks)


def displacement_kernel(w_ref, series_ref, *refs):
    blocks, (out_ref, held_ref, sem) = refs[:-3], refs[-3:]
    epochs, rows, cols = held_ref.shape
    deep = len(blocks) * blocks[0].shape[0] * SUB
    start = w_ref.shape[1] - deep
    parts = [slice(t * SUB, (t + 1) * SUB) for t in range(rows // SUB)]
    stacks = [stacked(blocks, part) for part in parts]
    copies = []
    for n, e in enumerate(range(0, epochs, CUT)):
        for part, stack in zip(parts, stacks):
            found = jnp.dot(w_ref[e * SUB : (e + CUT) * SUB, start:], stack, preferred_element_type=F32)
            found = found.reshape(CUT, SUB, cols) + series_ref[e : e + CUT, part, :]
            held_ref[e : e + CUT, part, :] = found.astype(BF16)
        copies.append(pltpu.make_async_copy(held_ref.at[e : e + CUT], out_ref.at[e : e + CUT], sem.at[n]))
        copies[-1].start()
    for copy in copies:
        copy.wait()


def banded(shape, axis, start):
    step = lax.broadcasted_iota(jnp.int32, shape, axis) - start
    step = step - lax.broadcasted_iota(jnp.int32, shape, 1 - axis)
    return jnp.where(jnp.abs(step) <= REACH, step, 0).astype(F32).astype(BF16)


def gradient_kernel(v_ref, right_ref, two_ref, one_ref, left_ref, rows_ref, cols_ref):
    rows, cols = v_ref.shape
    scale = (REACH * (REACH + 1) * (2 * REACH + 1) // 3) ** -0.5
    tile = lax.axis_index("grp") * lax.axis_size("row") + lax.axis_index("row")
    tiles = lax.axis_size("grp") * lax.axis_size("row")
    place, columns = lax.axis_index("col"), lax.axis_size("col")
    core, column = tile & 1, place & 1
    v = v_ref[...]
    one, two = one_ref[...], two_ref[...]
    above = jnp.where(tile == 0, 0.0, jnp.where(core == 0, two, one))
    below = jnp.where(tile == tiles - 1, 0.0, jnp.where(core == 0, one, two))
    upright = jnp.concatenate([above, v, below], axis=0)
    taps = banded((rows, rows + 2 * REACH), 1, REACH)
    total = jnp.zeros((rows, cols), F32)
    for part in three_parts(upright):
        total = total + jnp.dot(taps, part, preferred_element_type=F32)
    rows_ref[...] = total * scale
    first, second = left_ref[:rows, :], right_ref[:rows, :]
    before = jnp.where(place == 0, 0.0, jnp.where(column == 0, second, first))
    after = jnp.where(place == columns - 1, 0.0, jnp.where(column == 0, first, second))
    sideways = jnp.concatenate([before, v, after], axis=1)
    parts = jnp.concatenate(three_parts(sideways), axis=0)
    taps = banded((3 * LANES, LANES), 0, LANES)
    for c in range(0, cols, LANES):
        found = jnp.dot(parts[:, c : c + 3 * LANES], taps, preferred_element_type=F32)
        found = found[:rows] + found[rows : 2 * rows] + found[2 * rows :]
        cols_ref[:, c : c + LANES] = found * scale


VMEM = pl.BlockSpec(memory_space=pltpu.VMEM)


def call(kernel, inputs, outputs, flops, moved, limit=VMEM_BYTES, **more):
    return pl.pallas_call(
        kernel,
        in_specs=inputs,
        out_shape=outputs,
        cost_estimate=pl.CostEstimate(flops=flops, bytes_accessed=moved, transcendentals=0),
        compiler_params=pltpu.CompilerParams(vmem_limit_bytes=limit),
        **more,
    )


def shape(*dims, dtype=F32):
    return jax.ShapeDtypeStruct(dims, dtype)


def on_device(phase, pseudo_inverse, rotation, plate_id, coherent):
    share, groups, rows, cols = phase.shape
    epochs, ifg = pseudo_inverse.shape
    tiles = groups * lax.axis_size("row")
    both = ("grp", "row")
    tall, deep = epochs * SUB, ifg * SUB
    x, y, core = place_here()

    def cut(name):
        return lax.dynamic_index_in_dim(phase, partner(name, x, y, core, jnp.where), 1, keepdims=False)

    def send(names):
        return {name: lax.ppermute(cut(name), both, swap_pairs(name)) for name in names}

    got = send(EARLY + LATE[:1])
    later = (got[STARTS[0]], phase, pseudo_inverse, rotation, plate_id, coherent)
    got[STARTS[0]], phase, pseudo_inverse, rotation, plate_id, coherent = lax.optimization_barrier(later)
    got.update(send(LATE[1:]))
    early = [cut("own")] + [got[name] for name in EARLY]
    late = [got[name] for name in LATE]

    w, plate_rate, weight = call(
        prep_kernel,
        [VMEM, VMEM, VMEM],
        (shape(tall, deep, dtype=BF16), shape(rows, cols), shape(ifg, LANES)),
        2 * tall * deep * ifg,
        2 * tall * deep,
    )(rotation, pseudo_inverse, plate_id)

    series, rate = call(
        series_kernel,
        [VMEM] * (2 + len(early)),
        (shape(epochs, rows, cols), shape(rows, cols)),
        2 * epochs * ifg * rows * cols * SUB,
        2 * ifg * rows * cols,
    )(w, weight, *early)
    series, plate_rate = lax.optimization_barrier((series, plate_rate))

    velocity, one, two, left, right = call(
        rate_kernel,
        [VMEM] * (4 + len(late)),
        (shape(rows, cols), shape(REACH, cols), shape(REACH, cols), shape(rows + EXTRA, LANES), shape(rows, LANES)),
        2 * ifg * rows * cols,
        2 * ifg * rows * cols,
    )(weight, rate, *late, coherent, plate_rate)

    columns = lax.axis_size("col")
    everywhere = ("grp", "row", "col")
    right = lax.ppermute(right, everywhere, neighbour_pairs(tiles, columns, 1, 1))
    one = lax.ppermute(one, everywhere, neighbour_pairs(tiles, columns, 0, 0))
    two = lax.ppermute(two, everywhere, neighbour_pairs(tiles, columns, 0, 1))
    left = lax.ppermute(left, everywhere, neighbour_pairs(tiles, columns, 1, 0))
    displacement = call(
        displacement_kernel,
        [VMEM] * (2 + len(late)),
        shape(epochs, rows, cols, dtype=BF16),
        epochs * ifg * rows * cols * SUB,
        2 * epochs * rows * cols,
        out_specs=pl.BlockSpec(memory_space=pl.ANY),
        scratch_shapes=[
            pltpu.VMEM((epochs, rows, cols), BF16),
            pltpu.SemaphoreType.DMA((epochs // CUT,)),
        ],
    )(w, series, *late)

    grad_rows, grad_cols = call(
        gradient_kernel,
        [VMEM] * 5,
        (shape(rows, cols), shape(rows, cols)),
        2 * 200 * rows * cols,
        16 * rows * cols,
    )(velocity, right, two, one, left)
    return (displacement, grad_rows, grad_cols)


def solution(mesh):
    return jax.shard_map(
        on_device,
        mesh=mesh,
        in_specs=(
            P("grp", None, "row", "col"),
            P(),
            P(),
            P(("grp", "row"), "col"),
            P(("grp", "row"), "col"),
        ),
        out_specs=(
            P(None, ("grp", "row"), "col"),
            P(("grp", "row"), "col"),
            P(("grp", "row"), "col"),
        ),
        check_vma=False,
    )
```

```python
import math

import jax
import jax.numpy as jnp
from jax import lax
from jax.experimental import pallas as pl
from jax.experimental.pallas import tpu as pltpu
from jax.sharding import PartitionSpec as P

REACH = 16
SUB = 16
LANES = 128
F32 = jnp.float32
BF16 = jnp.bfloat16
VMEM_BYTES = 40 << 20
EXTRA = 8
CUT = 16

FLOWS = {
    "own": (0, 0),
    "D2": (2, 1),
    "Da": ("a", 1),
    "Db": ("b", 1),
    "X2": (2, 0),
    "Y2": (0, 1),
    "Xa": ("a", 0),
    "Xb": ("b", 0),
}
EARLY = ("D2", "Xb", "Da", "X2")
LATE = ("Db", "Y2", "Xa")
ORDER = ("own",) + EARLY + LATE
STARTS = EARLY + LATE


def along_x(step, x, core, pick):
    if step == "a":
        return pick(((x + core) & 1) == 0, 1, 3)
    if step == "b":
        return pick(((x + core) & 1) == 0, 3, 1)
    return step


def partner(flow, x, y, core, pick):
    step, turn = FLOWS[flow]
    return (((x + along_x(step, x, core, pick)) & 3) << 1) + ((y + turn) & 1)


def swap_pairs(flow):
    def choose(test, first, second):
        return first if test else second

    pairs = []
    for grp in range(8):
        for row in range(4):
            other = partner(flow, grp // 2, grp % 2, row % 2, choose)
            pairs.append((grp * 4 + row, other * 4 + row))
    return pairs


def neighbour_pairs(tiles, columns, along, first):
    pairs = []
    for tile in range(tiles):
        for column in range(columns):
            count = (tiles, columns)[along]
            here = (tile, column)[along]
            other = here + 1 if here % 2 == first else here - 1
            if 0 <= other < count:
                there = (other, column) if along == 0 else (tile, other)
            else:
                there = (tile, column ^ 1) if along == 0 else (tile ^ 1, column)
            pairs.append((tile * columns + column, there[0] * columns + there[1]))
    return pairs


def three_parts(value):
    high = value.astype(BF16)
    rest = value - high.astype(F32)
    mid = rest.astype(BF16)
    low = (rest - mid.astype(F32)).astype(BF16)
    return high, mid, low


def rate_weights(pinv_ref, weight_ref):
    epochs, ifg = pinv_ref.shape
    steps = lax.broadcasted_iota(jnp.int32, (epochs, LANES), 0).astype(F32) - (epochs - 1) / 2.0
    slope = steps * (epochs * (epochs * epochs - 1) / 12.0) ** -0.5
    total = jnp.zeros((ifg, LANES), F32)
    for part in three_parts(slope):
        total = total + lax.dot_general(
            pinv_ref[...], part, (((0,), (0,)), ((), ())), preferred_element_type=F32
        )
    weight_ref[...] = total


def prep_kernel(rot_ref, pinv_ref, plate_ref, w_ref, rate_ref, weight_ref):
    rate_weights(pinv_ref, weight_ref)
    epochs, ifg = pinv_ref.shape
    rows, cols = plate_ref.shape
    x, y, core = place_here()
    tall = epochs * SUB
    grow = lax.broadcasted_iota(jnp.int32, (tall, epochs), 0) // SUB
    pick = (grow == lax.broadcasted_iota(jnp.int32, (tall, epochs), 1)).astype(BF16)
    tall_inverse = jnp.dot(pick, pinv_ref[...], preferred_element_type=F32).astype(BF16)
    share = ifg // 8
    wide = share * SUB
    here = lax.broadcasted_iota(jnp.int32, (ifg, wide), 0)
    there = lax.broadcasted_iota(jnp.int32, (ifg, wide), 1) // SUB
    diagonal = (lax.broadcasted_iota(jnp.int32, (tall, wide), 0) % SUB) == (
        lax.broadcasted_iota(jnp.int32, (tall, wide), 1) % SUB
    )
    for k, name in enumerate(ORDER):
        source = partner(name, x, y, core, jnp.where)
        spread = (here == there + source * share).astype(BF16)
        block = jnp.dot(tall_inverse, spread, preferred_element_type=F32)
        w_ref[:, k * wide : (k + 1) * wide] = jnp.where(diagonal, block, 0.0).astype(BF16)
    tile = lax.axis_index("grp") * lax.axis_size("row") + lax.axis_index("row")
    total_rows = rows * lax.axis_size("grp") * lax.axis_size("row")
    total_cols = cols * lax.axis_size("col")
    down = lax.broadcasted_iota(jnp.int32, (rows, LANES), 0) + tile * rows
    over = lax.broadcasted_iota(jnp.int32, (8, cols), 1) + lax.axis_index("col") * cols
    lat = (36.0 + 6.0 * (down.astype(F32) + 0.5) / total_rows) * (math.pi / 180.0)
    lon = (26.0 + 19.0 * (over.astype(F32) + 0.5) / total_cols) * (math.pi / 180.0)
    cos_lat, sin_lat = jnp.cos(lat)[:, 0:1], jnp.sin(lat)[:, 0:1]
    cos_lon, sin_lon = jnp.cos(lon)[0:1, :], jnp.sin(lon)[0:1, :]
    sx, sy, sz = (0.38, -0.08, 0.92)
    px = cos_lat * cos_lon
    py = cos_lat * sin_lon
    pz = sin_lat + 0.0 * sin_lon
    lever = (py * sz - pz * sy, pz * sx - px * sz, px * sy - py * sx)
    plate = plate_ref[...]
    total = jnp.zeros(plate.shape, F32)
    for p in range(rot_ref.shape[0]):
        along = jnp.zeros(plate.shape, F32)
        for k in range(3):
            along = along + rot_ref[p : p + 1, k : k + 1] * lever[k]
        total = total + jnp.where(plate == p, along, 0.0)
    rate_ref[...] = total


def weighted(total, block, weight_ref, source):
    share, _, cols = block.shape
    for i in range(share):
        row = weight_ref[pl.ds(source * share + i, 1), :]
        total = total + jnp.concatenate([row] * (cols // LANES), axis=1) * block[i].astype(F32)
    return total


def place_here():
    grp, row = lax.axis_index("grp"), lax.axis_index("row")
    return grp >> 1, grp & 1, row & 1


def rates(total, weight_ref, names, blocks):
    x, y, core = place_here()
    for name, block in zip(names, blocks):
        total = weighted(total, block, weight_ref, partner(name, x, y, core, jnp.where))
    return total


def rate_kernel(weight_ref, part_ref, *refs):
    v_ref, one_ref, two_ref, left_ref, right_ref = refs[-5:]
    coherent_ref, plate_rate_ref = refs[-7:-5]
    rows, cols = v_ref.shape
    rate = rates(part_ref[...], weight_ref, LATE, refs[:-7])
    v_ref[...] = coherent_ref[...].astype(F32) * rate - plate_rate_ref[...]
    core = place_here()[2]
    column = lax.axis_index("col") & 1
    top, low = v_ref[:REACH, :], v_ref[rows - REACH :, :]
    first, last = v_ref[:, :LANES], v_ref[:, cols - LANES :]
    one_ref[...] = jnp.where(core == 0, low, top)
    two_ref[...] = jnp.where(core == 0, top, low)
    left_ref[:rows, :] = jnp.where(column == 0, last, first)
    left_ref[rows:, :] = jnp.zeros((EXTRA, LANES), F32)
    right_ref[:rows, :] = jnp.where(column == 0, first, last)


def stacked(blocks, part):
    share, _, cols = blocks[0].shape
    return jnp.concatenate([b[:, part, :].reshape(share * SUB, cols) for b in blocks], axis=0)


def series_kernel(w_ref, weight_ref, *refs):
    blocks, out_ref, rate_ref = refs[:-2], refs[-2], refs[-1]
    epochs, rows, cols = out_ref.shape
    deep = len(blocks) * blocks[0].shape[0] * SUB
    for t in range(rows // SUB):
        part = slice(t * SUB, (t + 1) * SUB)
        stack = stacked(blocks, part)
        for e in range(0, epochs, CUT):
            found = jnp.dot(w_ref[e * SUB : (e + CUT) * SUB, :deep], stack, preferred_element_type=F32)
            out_ref[e : e + CUT, part, :] = found.reshape(CUT, SUB, cols)
    rate_ref[...] = rates(jnp.zeros((rows, cols), F32), weight_ref, ("own",) + EARLY, blocks)


def displacement_kernel(w_ref, series_ref, *refs):
    blocks, (out_ref, held_ref, sem) = refs[:-3], refs[-3:]
    epochs, rows, cols = held_ref.shape
    deep = len(blocks) * blocks[0].shape[0] * SUB
    start = w_ref.shape[1] - deep
    parts = [slice(t * SUB, (t + 1) * SUB) for t in range(rows // SUB)]
    stacks = [stacked(blocks, part) for part in parts]
    copies = []
    for n, e in enumerate(range(0, epochs, CUT)):
        for part, stack in zip(parts, stacks):
            found = jnp.dot(w_ref[e * SUB : (e + CUT) * SUB, start:], stack, preferred_element_type=F32)
            found = found.reshape(CUT, SUB, cols) + series_ref[e : e + CUT, part, :]
            held_ref[e : e + CUT, part, :] = found.astype(BF16)
        copies.append(pltpu.make_async_copy(held_ref.at[e : e + CUT], out_ref.at[e : e + CUT], sem.at[n]))
        copies[-1].start()
    for copy in copies:
        copy.wait()


def banded(shape, axis, start):
    step = lax.broadcasted_iota(jnp.int32, shape, axis) - start
    step = step - lax.broadcasted_iota(jnp.int32, shape, 1 - axis)
    return jnp.where(jnp.abs(step) <= REACH, step, 0).astype(F32).astype(BF16)


def gradient_kernel(v_ref, right_ref, two_ref, one_ref, left_ref, rows_ref, cols_ref):
    rows, cols = v_ref.shape
    scale = (REACH * (REACH + 1) * (2 * REACH + 1) // 3) ** -0.5
    tile = lax.axis_index("grp") * lax.axis_size("row") + lax.axis_index("row")
    tiles = lax.axis_size("grp") * lax.axis_size("row")
    place, columns = lax.axis_index("col"), lax.axis_size("col")
    core, column = tile & 1, place & 1
    v = v_ref[...]
    one, two = one_ref[...], two_ref[...]
    above = jnp.where(tile == 0, 0.0, jnp.where(core == 0, two, one))
    below = jnp.where(tile == tiles - 1, 0.0, jnp.where(core == 0, one, two))
    upright = jnp.concatenate([above, v, below], axis=0)
    taps = banded((rows, rows + 2 * REACH), 1, REACH)
    total = jnp.zeros((rows, cols), F32)
    for part in three_parts(upright):
        total = total + jnp.dot(taps, part, preferred_element_type=F32)
    rows_ref[...] = total * scale
    first, second = left_ref[:rows, :], right_ref[:rows, :]
    before = jnp.where(place == 0, 0.0, jnp.where(column == 0, second, first))
    after = jnp.where(place == columns - 1, 0.0, jnp.where(column == 0, first, second))
    sideways = jnp.concatenate([before, v, after], axis=1)
    parts = jnp.concatenate(three_parts(sideways), axis=0)
    taps = banded((3 * LANES, LANES), 0, LANES)
    for c in range(0, cols, LANES):
        found = jnp.dot(parts[:, c : c + 3 * LANES], taps, preferred_element_type=F32)
        found = found[:rows] + found[rows : 2 * rows] + found[2 * rows :]
        cols_ref[:, c : c + LANES] = found * scale


VMEM = pl.BlockSpec(memory_space=pltpu.VMEM)


def call(kernel, inputs, outputs, flops, moved, limit=VMEM_BYTES, **more):
    return pl.pallas_call(
        kernel,
        in_specs=inputs,
        out_shape=outputs,
        cost_estimate=pl.CostEstimate(flops=flops, bytes_accessed=moved, transcendentals=0),
        compiler_params=pltpu.CompilerParams(vmem_limit_bytes=limit),
        **more,
    )


def shape(*dims, dtype=F32):
    return jax.ShapeDtypeStruct(dims, dtype)


def on_device(phase, pseudo_inverse, rotation, plate_id, coherent):
    share, groups, rows, cols = phase.shape
    epochs, ifg = pseudo_inverse.shape
    tiles = groups * lax.axis_size("row")
    both = ("grp", "row")
    tall, deep = epochs * SUB, ifg * SUB
    x, y, core = place_here()

    def cut(name):
        return lax.dynamic_index_in_dim(phase, partner(name, x, y, core, jnp.where), 1, keepdims=False)

    def send(names):
        return {name: lax.ppermute(cut(name), both, swap_pairs(name)) for name in names}

    got = send(EARLY + LATE[:1])
    later = (got[STARTS[0]], phase, pseudo_inverse, rotation, plate_id, coherent)
    got[STARTS[0]], phase, pseudo_inverse, rotation, plate_id, coherent = lax.optimization_barrier(later)
    got.update(send(LATE[1:]))
    early = [cut("own")] + [got[name] for name in EARLY]
    late = [got[name] for name in LATE]

    w, plate_rate, weight = call(
        prep_kernel,
        [VMEM, VMEM, VMEM],
        (shape(tall, deep, dtype=BF16), shape(rows, cols), shape(ifg, LANES)),
        2 * tall * deep * ifg,
        2 * tall * deep,
    )(rotation, pseudo_inverse, plate_id)

    series, rate = call(
        series_kernel,
        [VMEM] * (2 + len(early)),
        (shape(epochs, rows, cols), shape(rows, cols)),
        2 * epochs * ifg * rows * cols * SUB,
        2 * ifg * rows * cols,
    )(w, weight, *early)
    series, plate_rate = lax.optimization_barrier((series, plate_rate))

    velocity, one, two, left, right = call(
        rate_kernel,
        [VMEM] * (4 + len(late)),
        (shape(rows, cols), shape(REACH, cols), shape(REACH, cols), shape(rows + EXTRA, LANES), shape(rows, LANES)),
        2 * ifg * rows * cols,
        2 * ifg * rows * cols,
    )(weight, rate, *late, coherent, plate_rate)

    columns = lax.axis_size("col")
    everywhere = ("grp", "row", "col")
    right = lax.ppermute(right, everywhere, neighbour_pairs(tiles, columns, 1, 1))
    one = lax.ppermute(one, everywhere, neighbour_pairs(tiles, columns, 0, 0))
    two = lax.ppermute(two, everywhere, neighbour_pairs(tiles, columns, 0, 1))
    left = lax.ppermute(left, everywhere, neighbour_pairs(tiles, columns, 1, 0))
    displacement = call(
        displacement_kernel,
        [VMEM] * (2 + len(late)),
        shape(epochs, rows, cols, dtype=BF16),
        epochs * ifg * rows * cols * SUB,
        2 * epochs * rows * cols,
        out_specs=pl.BlockSpec(memory_space=pl.ANY),
        scratch_shapes=[
            pltpu.VMEM((epochs, rows, cols), BF16),
            pltpu.SemaphoreType.DMA((epochs // CUT,)),
        ],
    )(w, series, *late)

    grad_rows, grad_cols = call(
        gradient_kernel,
        [VMEM] * 5,
        (shape(rows, cols), shape(rows, cols)),
        2 * 200 * rows * cols,
        16 * rows * cols,
    )(velocity, right, two, one, left)
    return (displacement, grad_rows, grad_cols)


def solution(mesh):
    return jax.shard_map(
        on_device,
        mesh=mesh,
        in_specs=(
            P("grp", None, "row", "col"),
            P(),
            P(),
            P(("grp", "row"), "col"),
            P(("grp", "row"), "col"),
        ),
        out_specs=(
            P(None, ("grp", "row"), "col"),
            P(("grp", "row"), "col"),
            P(("grp", "row"), "col"),
        ),
        check_vma=False,
    )
```

```python
import math

import jax
import jax.numpy as jnp
from jax import lax
from jax.experimental import pallas as pl
from jax.experimental.pallas import tpu as pltpu
from jax.sharding import PartitionSpec as P

REACH = 16
SUB = 16
LANES = 128
F32 = jnp.float32
BF16 = jnp.bfloat16
VMEM_BYTES = 40 << 20
EXTRA = 8
CUT = 16

FLOWS = {
    "own": (0, 0),
    "D2": (2, 1),
    "Da": ("a", 1),
    "Db": ("b", 1),
    "X2": (2, 0),
    "Y2": (0, 1),
    "Xa": ("a", 0),
    "Xb": ("b", 0),
}
EARLY = ("D2", "Xb", "Da", "X2")
LATE = ("Db", "Y2", "Xa")
ORDER = ("own",) + EARLY + LATE
STARTS = EARLY + LATE


def along_x(step, x, core, pick):
    if step == "a":
        return pick(((x + core) & 1) == 0, 1, 3)
    if step == "b":
        return pick(((x + core) & 1) == 0, 3, 1)
    return step


def partner(flow, x, y, core, pick):
    step, turn = FLOWS[flow]
    return (((x + along_x(step, x, core, pick)) & 3) << 1) + ((y + turn) & 1)


def swap_pairs(flow):
    def choose(test, first, second):
        return first if test else second

    pairs = []
    for grp in range(8):
        for row in range(4):
            other = partner(flow, grp // 2, grp % 2, row % 2, choose)
            pairs.append((grp * 4 + row, other * 4 + row))
    return pairs


def neighbour_pairs(tiles, columns, along, first):
    pairs = []
    for tile in range(tiles):
        for column in range(columns):
            count = (tiles, columns)[along]
            here = (tile, column)[along]
            other = here + 1 if here % 2 == first else here - 1
            if 0 <= other < count:
                there = (other, column) if along == 0 else (tile, other)
            else:
                there = (tile, column ^ 1) if along == 0 else (tile ^ 1, column)
            pairs.append((tile * columns + column, there[0] * columns + there[1]))
    return pairs


def three_parts(value):
    high = value.astype(BF16)
    rest = value - high.astype(F32)
    mid = rest.astype(BF16)
    low = (rest - mid.astype(F32)).astype(BF16)
    return high, mid, low


def rate_weights(pinv_ref, weight_ref):
    epochs, ifg = pinv_ref.shape
    steps = lax.broadcasted_iota(jnp.int32, (epochs, LANES), 0).astype(F32) - (epochs - 1) / 2.0
    slope = steps * (epochs * (epochs * epochs - 1) / 12.0) ** -0.5
    total = jnp.zeros((ifg, LANES), F32)
    for part in three_parts(slope):
        total = total + lax.dot_general(
            pinv_ref[...], part, (((0,), (0,)), ((), ())), preferred_element_type=F32
        )
    weight_ref[...] = total


def prep_kernel(rot_ref, pinv_ref, plate_ref, w_ref, rate_ref, weight_ref):
    rate_weights(pinv_ref, weight_ref)
    epochs, ifg = pinv_ref.shape
    rows, cols = plate_ref.shape
    x, y, core = place_here()
    tall = epochs * SUB
    grow = lax.broadcasted_iota(jnp.int32, (tall, epochs), 0) // SUB
    pick = (grow == lax.broadcasted_iota(jnp.int32, (tall, epochs), 1)).astype(BF16)
    tall_inverse = jnp.dot(pick, pinv_ref[...], preferred_element_type=F32).astype(BF16)
    share = ifg // 8
    wide = share * SUB
    here = lax.broadcasted_iota(jnp.int32, (ifg, wide), 0)
    there = lax.broadcasted_iota(jnp.int32, (ifg, wide), 1) // SUB
    diagonal = (lax.broadcasted_iota(jnp.int32, (tall, wide), 0) % SUB) == (
        lax.broadcasted_iota(jnp.int32, (tall, wide), 1) % SUB
    )
    for k, name in enumerate(ORDER):
        source = partner(name, x, y, core, jnp.where)
        spread = (here == there + source * share).astype(BF16)
        block = jnp.dot(tall_inverse, spread, preferred_element_type=F32)
        w_ref[:, k * wide : (k + 1) * wide] = jnp.where(diagonal, block, 0.0).astype(BF16)
    tile = lax.axis_index("grp") * lax.axis_size("row") + lax.axis_index("row")
    total_rows = rows * lax.axis_size("grp") * lax.axis_size("row")
    total_cols = cols * lax.axis_size("col")
    down = lax.broadcasted_iota(jnp.int32, (rows, LANES), 0) + tile * rows
    over = lax.broadcasted_iota(jnp.int32, (8, cols), 1) + lax.axis_index("col") * cols
    lat = (36.0 + 6.0 * (down.astype(F32) + 0.5) / total_rows) * (math.pi / 180.0)
    lon = (26.0 + 19.0 * (over.astype(F32) + 0.5) / total_cols) * (math.pi / 180.0)
    cos_lat, sin_lat = jnp.cos(lat)[:, 0:1], jnp.sin(lat)[:, 0:1]
    cos_lon, sin_lon = jnp.cos(lon)[0:1, :], jnp.sin(lon)[0:1, :]
    sx, sy, sz = (0.38, -0.08, 0.92)
    px = cos_lat * cos_lon
    py = cos_lat * sin_lon
    pz = sin_lat + 0.0 * sin_lon
    lever = (py * sz - pz * sy, pz * sx - px * sz, px * sy - py * sx)
    plate = plate_ref[...]
    total = jnp.zeros(plate.shape, F32)
    for p in range(rot_ref.shape[0]):
        along = jnp.zeros(plate.shape, F32)
        for k in range(3):
            along = along + rot_ref[p : p + 1, k : k + 1] * lever[k]
        total = total + jnp.where(plate == p, along, 0.0)
    rate_ref[...] = total


def weighted(total, block, weight_ref, source):
    share, _, cols = block.shape
    for i in range(share):
        row = weight_ref[pl.ds(source * share + i, 1), :]
        total = total + jnp.concatenate([row] * (cols // LANES), axis=1) * block[i].astype(F32)
    return total


def place_here():
    grp, row = lax.axis_index("grp"), lax.axis_index("row")
    return grp >> 1, grp & 1, row & 1


def rates(total, weight_ref, names, blocks):
    x, y, core = place_here()
    for name, block in zip(names, blocks):
        total = weighted(total, block, weight_ref, partner(name, x, y, core, jnp.where))
    return total


def rate_kernel(weight_ref, part_ref, *refs):
    v_ref, one_ref, two_ref, left_ref, right_ref = refs[-5:]
    coherent_ref, plate_rate_ref = refs[-7:-5]
    rows, cols = v_ref.shape
    rate = rates(part_ref[...], weight_ref, LATE, refs[:-7])
    v_ref[...] = coherent_ref[...].astype(F32) * rate - plate_rate_ref[...]
    core = place_here()[2]
    column = lax.axis_index("col") & 1
    top, low = v_ref[:REACH, :], v_ref[rows - REACH :, :]
    first, last = v_ref[:, :LANES], v_ref[:, cols - LANES :]
    one_ref[...] = jnp.where(core == 0, low, top)
    two_ref[...] = jnp.where(core == 0, top, low)
    left_ref[:rows, :] = jnp.where(column == 0, last, first)
    left_ref[rows:, :] = jnp.zeros((EXTRA, LANES), F32)
    right_ref[:rows, :] = jnp.where(column == 0, first, last)


def stacked(blocks, part):
    share, _, cols = blocks[0].shape
    return jnp.concatenate([b[:, part, :].reshape(share * SUB, cols) for b in blocks], axis=0)


def series_kernel(w_ref, weight_ref, *refs):
    blocks, out_ref, rate_ref = refs[:-2], refs[-2], refs[-1]
    epochs, rows, cols = out_ref.shape
    deep = len(blocks) * blocks[0].shape[0] * SUB
    for t in range(rows // SUB):
        part = slice(t * SUB, (t + 1) * SUB)
        stack = stacked(blocks, part)
        for e in range(0, epochs, CUT):
            found = jnp.dot(w_ref[e * SUB : (e + CUT) * SUB, :deep], stack, preferred_element_type=F32)
            out_ref[e : e + CUT, part, :] = found.reshape(CUT, SUB, cols)
    rate_ref[...] = rates(jnp.zeros((rows, cols), F32), weight_ref, ("own",) + EARLY, blocks)


def displacement_kernel(w_ref, series_ref, *refs):
    blocks, (out_ref, held_ref, sem) = refs[:-3], refs[-3:]
    epochs, rows, cols = held_ref.shape
    deep = len(blocks) * blocks[0].shape[0] * SUB
    start = w_ref.shape[1] - deep
    copies = []
    for t in range(rows // SUB):
        part = slice(t * SUB, (t + 1) * SUB)
        found = jnp.dot(w_ref[:, start:], stacked(blocks, part), preferred_element_type=F32)
        found = found.reshape(epochs, SUB, cols) + series_ref[:, part, :]
        held_ref[:, part, :] = found.astype(BF16)
        copies.append(pltpu.make_async_copy(held_ref.at[:, part], out_ref.at[:, part], sem.at[t]))
        copies[-1].start()
    for copy in copies:
        copy.wait()


def banded(shape, axis, start):
    step = lax.broadcasted_iota(jnp.int32, shape, axis) - start
    step = step - lax.broadcasted_iota(jnp.int32, shape, 1 - axis)
    return jnp.where(jnp.abs(step) <= REACH, step, 0).astype(F32).astype(BF16)


def gradient_kernel(v_ref, right_ref, two_ref, one_ref, left_ref, rows_ref, cols_ref):
    rows, cols = v_ref.shape
    scale = (REACH * (REACH + 1) * (2 * REACH + 1) // 3) ** -0.5
    tile = lax.axis_index("grp") * lax.axis_size("row") + lax.axis_index("row")
    tiles = lax.axis_size("grp") * lax.axis_size("row")
    place, columns = lax.axis_index("col"), lax.axis_size("col")
    core, column = tile & 1, place & 1
    v = v_ref[...]
    one, two = one_ref[...], two_ref[...]
    above = jnp.where(tile == 0, 0.0, jnp.where(core == 0, two, one))
    below = jnp.where(tile == tiles - 1, 0.0, jnp.where(core == 0, one, two))
    upright = jnp.concatenate([above, v, below], axis=0)
    taps = banded((rows, rows + 2 * REACH), 1, REACH)
    total = jnp.zeros((rows, cols), F32)
    for part in three_parts(upright):
        total = total + jnp.dot(taps, part, preferred_element_type=F32)
    rows_ref[...] = total * scale
    first, second = left_ref[:rows, :], right_ref[:rows, :]
    before = jnp.where(place == 0, 0.0, jnp.where(column == 0, second, first))
    after = jnp.where(place == columns - 1, 0.0, jnp.where(column == 0, first, second))
    sideways = jnp.concatenate([before, v, after], axis=1)
    parts = jnp.concatenate(three_parts(sideways), axis=0)
    taps = banded((3 * LANES, LANES), 0, LANES)
    for c in range(0, cols, LANES):
        found = jnp.dot(parts[:, c : c + 3 * LANES], taps, preferred_element_type=F32)
        found = found[:rows] + found[rows : 2 * rows] + found[2 * rows :]
        cols_ref[:, c : c + LANES] = found * scale


VMEM = pl.BlockSpec(memory_space=pltpu.VMEM)


def call(kernel, inputs, outputs, flops, moved, limit=VMEM_BYTES, **more):
    return pl.pallas_call(
        kernel,
        in_specs=inputs,
        out_shape=outputs,
        cost_estimate=pl.CostEstimate(flops=flops, bytes_accessed=moved, transcendentals=0),
        compiler_params=pltpu.CompilerParams(vmem_limit_bytes=limit),
        **more,
    )


def shape(*dims, dtype=F32):
    return jax.ShapeDtypeStruct(dims, dtype)


def on_device(phase, pseudo_inverse, rotation, plate_id, coherent):
    share, groups, rows, cols = phase.shape
    epochs, ifg = pseudo_inverse.shape
    tiles = groups * lax.axis_size("row")
    both = ("grp", "row")
    tall, deep = epochs * SUB, ifg * SUB
    x, y, core = place_here()

    def cut(name):
        return lax.dynamic_index_in_dim(phase, partner(name, x, y, core, jnp.where), 1, keepdims=False)

    def send(names):
        return {name: lax.ppermute(cut(name), both, swap_pairs(name)) for name in names}

    got = send(EARLY + LATE[:1])
    later = (got[STARTS[0]], phase, pseudo_inverse, rotation, plate_id, coherent)
    got[STARTS[0]], phase, pseudo_inverse, rotation, plate_id, coherent = lax.optimization_barrier(later)
    got.update(send(LATE[1:]))
    early = [cut("own")] + [got[name] for name in EARLY]
    late = [got[name] for name in LATE]

    w, plate_rate, weight = call(
        prep_kernel,
        [VMEM, VMEM, VMEM],
        (shape(tall, deep, dtype=BF16), shape(rows, cols), shape(ifg, LANES)),
        2 * tall * deep * ifg,
        2 * tall * deep,
    )(rotation, pseudo_inverse, plate_id)

    series, rate = call(
        series_kernel,
        [VMEM] * (2 + len(early)),
        (shape(epochs, rows, cols), shape(rows, cols)),
        2 * epochs * ifg * rows * cols * SUB,
        2 * ifg * rows * cols,
    )(w, weight, *early)
    series, plate_rate = lax.optimization_barrier((series, plate_rate))

    velocity, one, two, left, right = call(
        rate_kernel,
        [VMEM] * (4 + len(late)),
        (shape(rows, cols), shape(REACH, cols), shape(REACH, cols), shape(rows + EXTRA, LANES), shape(rows, LANES)),
        2 * ifg * rows * cols,
        2 * ifg * rows * cols,
    )(weight, rate, *late, coherent, plate_rate)

    columns = lax.axis_size("col")
    everywhere = ("grp", "row", "col")
    right = lax.ppermute(right, everywhere, neighbour_pairs(tiles, columns, 1, 1))
    one = lax.ppermute(one, everywhere, neighbour_pairs(tiles, columns, 0, 0))
    two = lax.ppermute(two, everywhere, neighbour_pairs(tiles, columns, 0, 1))
    left = lax.ppermute(left, everywhere, neighbour_pairs(tiles, columns, 1, 0))
    displacement = call(
        displacement_kernel,
        [VMEM] * (2 + len(late)),
        shape(epochs, rows, cols, dtype=BF16),
        epochs * ifg * rows * cols * SUB,
        2 * epochs * rows * cols,
        out_specs=pl.BlockSpec(memory_space=pl.ANY),
        scratch_shapes=[
            pltpu.VMEM((epochs, rows, cols), BF16),
            pltpu.SemaphoreType.DMA((rows // SUB,)),
        ],
    )(w, series, *late)

    grad_rows, grad_cols = call(
        gradient_kernel,
        [VMEM] * 5,
        (shape(rows, cols), shape(rows, cols)),
        2 * 200 * rows * cols,
        16 * rows * cols,
    )(velocity, right, two, one, left)
    return (displacement, grad_rows, grad_cols)


def solution(mesh):
    return jax.shard_map(
        on_device,
        mesh=mesh,
        in_specs=(
            P("grp", None, "row", "col"),
            P(),
            P(),
            P(("grp", "row"), "col"),
            P(("grp", "row"), "col"),
        ),
        out_specs=(
            P(None, ("grp", "row"), "col"),
            P(("grp", "row"), "col"),
            P(("grp", "row"), "col"),
        ),
        check_vma=False,
    )
```
